256 devices in a mesh: energy: 64 (over y, z, x_hi), slab: 4 (over x_lo, core).
Axes of the slice: x: 4 (x_hi: 2, x_lo: 2; x = x_hi * 2 + x_lo), y: 4, z: 8, core: 2. Of those that a mesh axis runs over, the one named last changes fastest.
Arguments:
- lesser: bfloat16 [64, 4, 2, 1024, 1024], P('energy', 'slab'), may hold values from -6 to 6
- greater_diag: float32 [64, 4, 1024], P('energy', 'slab'), may hold values from -6 to 6
- dipole: bfloat16 [4, 1024, 1024], P('slab'), may hold values from -0.1875 to 0.1875
- photon_weights: float32 [64, 3], P('energy'), may hold values from 0.2 to 1
- sidebands: int32 [64], P('energy'), may hold values from 1 to 2
- phonon_lags: int32 [6], replicated, may hold values from 1 to 31
- phonon_strengths: float32 [2, 6], replicated, may hold values from 0.3 to 1.5
- slab_coupling: float32 [4, 1024], P('slab'), may hold values from 0.3 to 1
Outputs:
- lesser_self: bfloat16 [64, 4, 2, 1024, 1024], P('energy', 'slab')
- greater_phonon: float32 [64, 4, 1024], P('energy', 'slab')
The draws below stay inside these ranges and needn't reach their ends.
All inputs are finite; a program needn't handle non-finite values.
Results may differ from the reference program's by a relative error of at most 0.0057.
Values may be sent and summed in bfloat16 or wider, within the bound.
A program may use at most 64 MiB of HBM per device.

```python
import math
import jax
import jax.numpy as jnp
from jax import lax

NORB = 1024
MODES = 6
NE = 64
PHOT = 3
SLABS = 4


def plant(result, key, low, top_value):
    longest = result.shape.index(max(result.shape))
    spots = []
    for shift in (0, 1):
        where = [jax.random.randint(jax.random.fold_in(key, axis), (), 0, length) for axis, length in enumerate(result.shape)]
        where[longest] = (where[longest] + shift) % result.shape[longest]
        spots.append(tuple(where))
    return result.at[spots[0]].set(low).at[spots[1]].set(top_value)


def levels(key, extent, pieces, least, largest):
    def one(position, blocks):
        draws = jax.random.uniform(jax.random.fold_in(jax.random.fold_in(key, 6), position), (blocks,), jnp.float32, least / len(pieces), largest / len(pieces))
        return jnp.repeat(jnp.exp(draws), extent[position] // blocks).reshape((-1,) + (1,) * (len(extent) - position - 1))

    loudness = one(*pieces[0])
    for cut in pieces[1:]:
        loudness = loudness * one(*cut)
    return loudness


def normal_values(own_key, extent, deviation, bound, split=(), kind=jnp.bfloat16):
    drawn = deviation * jax.random.normal(own_key, extent, jnp.float32)
    if split:
        drawn = drawn * levels(own_key, extent, split, -0.22, 0.18)
    return jnp.clip(drawn, -bound, bound).astype(kind)


def setup_inputs(seed: int = 0) -> dict:
    splits = jax.random.split(jax.random.key(seed), 9)
    lesser = normal_values(splits[0], (NE, SLABS, 2, NORB, NORB), 1.0, 6.0, ((0, 64), (1, 4)))
    greater_diag = normal_values(splits[1], (NE, SLABS, NORB), 1.0, 6.0, ((0, 64), (1, 4)), jnp.float32)
    dipole = normal_values(splits[2], (SLABS, NORB, NORB), NORB ** -0.5, 0.1875, ((0, 4),))
    photon_weights = jnp.clip(jnp.exp(math.log(1.0) - 1.609438 * jax.random.uniform(splits[3], (NE, 3), jnp.float32) ** levels(splits[3], (NE, 3), ((0, 64),), -0.2, 0.2)), 0.2, 1.0)
    sidebands = plant(jax.random.randint(splits[4], (NE,), 1, 3), jax.random.fold_in(splits[4], 1), 1, 2).astype(jnp.int32)
    phonon_lags = plant(jax.random.randint(splits[5], (MODES,), 1, NE // 2), jax.random.fold_in(splits[5], 1), 1, (NE // 2) - 1).astype(jnp.int32)
    phonon_strengths = jnp.clip(jnp.exp(jax.random.uniform(splits[6], (2, MODES), jnp.float32, math.log(0.3), math.log(1.5))), 0.3, 1.5)
    slab_coupling = jnp.clip(jnp.exp(math.log(1.0) - 1.2039728 * jax.random.uniform(splits[7], (SLABS, NORB), jnp.float32) ** levels(splits[7], (SLABS, NORB), ((0, 4),), -0.2, 0.2)), 0.3, 1.0)
    return {"lesser": lesser, "greater_diag": greater_diag, "dipole": dipole, "photon_weights": photon_weights, "sidebands": sidebands, "phonon_lags": phonon_lags, "phonon_strengths": phonon_strengths, "slab_coupling": slab_coupling}


def kernel(rows, cols, phonon_lags, first, second):
    offset = cols[None, :] - rows[:, None]
    upward = (offset[None, :, :] == phonon_lags[:, None, None]).astype(jnp.float32)
    downward = (offset[None, :, :] == -phonon_lags[:, None, None]).astype(jnp.float32)
    return jnp.sum(first[:, None, None] * upward + second[:, None, None] * downward, axis=0)


def couple(values, slab_coupling):
    scaled = slab_coupling[None] * values
    zeros = jnp.zeros_like(values[:, :1])
    below = jnp.concatenate([zeros, scaled[:, :-1]], axis=1)
    above = jnp.concatenate([values[:, 1:], zeros], axis=1)
    return values + below + slab_coupling[None] * above


def reference(lesser, greater_diag, dipole, photon_weights, sidebands, phonon_lags, phonon_strengths, slab_coupling):
    dip_wide = dipole.astype(jnp.float32)
    energies = jnp.arange(NE, dtype=jnp.int32)
    diag_less = jnp.diagonal(lesser[:, :, 1], axis1=-2, axis2=-1).astype(jnp.float32)
    k_less = kernel(energies, energies, phonon_lags, phonon_strengths[0], phonon_strengths[1])
    k_great = kernel(energies, energies, phonon_lags, phonon_strengths[1], phonon_strengths[0])
    corr_less = jnp.einsum('ef,fsn->esn', k_less, diag_less, precision=lax.Precision.HIGHEST)
    corr_great = jnp.einsum('ef,fsn->esn', k_great, greater_diag, precision=lax.Precision.HIGHEST)
    phon_less = couple(corr_less, slab_coupling)
    greater_phonon = couple(corr_great, slab_coupling)

    def left_product(block):
        return jnp.einsum('scij,skj->scik', block.astype(jnp.float32), dip_wide).astype(jnp.bfloat16)

    left = lax.map(left_product, lesser)
    masks = sidebands.astype(jnp.float32)
    eye_mask = (jnp.arange(NORB)[:, None] == jnp.arange(NORB)[None, :]).astype(jnp.float32)

    def per_energy(index):
        own_left = lax.dynamic_index_in_dim(left, index, 0, keepdims=False).astype(jnp.float32)
        lower = lax.dynamic_index_in_dim(left, jnp.maximum(index - PHOT, 0), 0, keepdims=False).astype(jnp.float32)
        upper = lax.dynamic_index_in_dim(left, jnp.minimum(index + PHOT, NE - 1), 0, keepdims=False).astype(jnp.float32)
        lower = jnp.where(index >= PHOT, lower, jnp.zeros_like(lower))
        upper = jnp.where(index + PHOT < NE, upper, jnp.zeros_like(upper))
        weights = lax.dynamic_index_in_dim(photon_weights, index, 0, keepdims=False)
        flag = lax.dynamic_index_in_dim(masks, index, 0, keepdims=False)
        mixed = (weights[0] * own_left + flag * (weights[1] * lower + weights[2] * upper)).astype(jnp.bfloat16)
        photon = jnp.einsum('sij,scjk->scik', dip_wide, mixed.astype(jnp.float32))
        diag_add = lax.dynamic_index_in_dim(phon_less, index, 0, keepdims=False)
        photon = photon.at[:, 1].add(eye_mask[None] * diag_add[:, :, None])
        return photon.astype(jnp.bfloat16)

    lesser_self = lax.map(per_energy, energies)
    return lesser_self, greater_phonon
```

```python
import jax
import jax.numpy as jnp
from jax import lax
from jax.experimental import pallas as pl
from jax.experimental.pallas import tpu as pltpu
from jax.sharding import PartitionSpec as P

F32, BF16 = jnp.float32, jnp.bfloat16
MESH = pl.DeviceIdType.MESH

RING = 8
LAYERS = 4
CHAIN = RING * LAYERS
SLABS = 4
MODES = 6
NORB = 1024
ROWS = 128
CHUNKS = NORB // ROWS
LAG = 2
BLOCK = 256
LANE = 128

CROSS, LOW, HIGH, BLOW, BHIGH, SUMS = range(6)


def body(
    lesser, great, dip, weights, flags, lags, strengths, coupling,
    out, great_out,
    g_v, d_v, crossed, low, high, blow, bhigh, sums, sums_out, left, acc, stage,
    zbuf, pbuf, qbuf, nbuf, nsend, phon, wsend, wrecv,
    send, recv, zs, zr, ps, pr, ns, nr, ws, wr, local, osem,
):
    e = lax.axis_index("energy")
    s = lax.axis_index("slab")
    w, h = e // 2, e % 2
    y, z = w // RING, w % RING
    mirror = (w * 2 + (1 - h), s)

    def at(chain):
        return (chain * 2 + h, s)

    def inside(chain):
        return jnp.logical_and(chain >= 0, chain < CHAIN)

    a_low, a_high = h - 2, h + 1
    b_low, b_high = -1 - h, 2 - h

    copies_in = [
        pltpu.make_async_copy(lesser.at[1], g_v.at[1], local.at[0]),
        pltpu.make_async_copy(lesser.at[0], g_v.at[0], local.at[1]),
        pltpu.make_async_copy(dip, d_v, local.at[2]),
    ]
    for copy in copies_in:
        copy.start()

    barrier = pltpu.get_barrier_semaphore()
    expected = jnp.int32(2 * (RING - 1))
    for step in (-2, -1, 1, 2):
        ok = inside(w + step)
        expected = expected + ok.astype(jnp.int32)

        @pl.when(ok)
        def _():
            pl.semaphore_signal(barrier, inc=1, device_id=at(w + step), device_id_type=MESH)

    def ring_mate(d):
        return ((y * RING + (z + d) % RING) * 2 + h, s)

    def plane_mate(t):
        return ((((y + t // 2) % LAYERS) * RING + z) * 2 + (h + t % 2) % 2, s)

    for d in range(1, RING):
        pl.semaphore_signal(barrier, inc=1, device_id=ring_mate(d), device_id_type=MESH)
        pl.semaphore_signal(barrier, inc=1, device_id=plane_mate(d), device_id_type=MESH)
    for step in (-1, 1):
        ok = jnp.logical_and(s + step >= 0, s + step < SLABS)
        expected = expected + ok.astype(jnp.int32)

        @pl.when(ok)
        def _():
            pl.semaphore_signal(barrier, inc=1, device_id=(e, s + step), device_id_type=MESH)

    pl.semaphore_wait(barrier, expected)

    def chunk_copy(stream, k):
        source, target, device = {
            CROSS: (lesser.at[0, pl.ds(k * ROWS, ROWS)], crossed.at[k], mirror),
            LOW: (crossed.at[k], low.at[k], at(w - a_low)),
            HIGH: (crossed.at[k], high.at[k], at(w - a_high)),
            BLOW: (lesser.at[1, pl.ds(k * ROWS, ROWS)], blow.at[k], at(w - b_low)),
            BHIGH: (lesser.at[1, pl.ds(k * ROWS, ROWS)], bhigh.at[k], at(w - b_high)),
            SUMS: (sums_out.at[k], sums.at[k], mirror),
        }[stream]
        return pltpu.make_async_remote_copy(
            source, target, send.at[stream, k], recv.at[stream, k],
            device_id=device, device_id_type=MESH,
        )

    sends_to = {
        LOW: inside(w - a_low), HIGH: inside(w - a_high),
        BLOW: inside(w - b_low), BHIGH: inside(w - b_high),
    }
    hears = {
        LOW: inside(w + a_low), HIGH: inside(w + a_high),
        BLOW: inside(w + b_low), BHIGH: inside(w + b_high),
    }

    def start(stream, k):
        if stream in sends_to:

            @pl.when(sends_to[stream])
            def _():
                chunk_copy(stream, k).start()
        else:
            chunk_copy(stream, k).start()

    def arrive(stream, k):
        if stream in hears:

            @pl.when(hears[stream])
            def _():
                chunk_copy(stream, k).wait_recv()
        else:
            chunk_copy(stream, k).wait_recv()

    def sent(stream, k):
        if stream in sends_to:

            @pl.when(sends_to[stream])
            def _():
                chunk_copy(stream, k).wait_send()
        else:
            chunk_copy(stream, k).wait_send()

    flag = flags[0].astype(F32)
    own_w, low_w, high_w = weights[0, 0], flag * weights[0, 1], flag * weights[0, 2]
    wsend[0] = jnp.full((8, LANE), low_w, F32)
    wsend[1] = jnp.full((8, LANE), high_w, F32)
    weight_copy = pltpu.make_async_remote_copy(
        wsend, wrecv, ws, wr, device_id=mirror, device_id_type=MESH
    )
    weight_copy.start()

    @pl.loop(0, CHUNKS)
    def _(k):
        start(BHIGH, k)
        start(BLOW, k)
        start(CROSS, k)

    for stream, buffer in ((LOW, low), (HIGH, high), (BLOW, blow), (BHIGH, bhigh)):

        @pl.when(jnp.logical_not(hears[stream]))
        def _():
            @pl.loop(0, CHUNKS)
            def _(k):
                buffer[k] = jnp.zeros((ROWS, NORB), BF16)

    eye = lax.broadcasted_iota(jnp.int32, (LANE, LANE), 0) == lax.broadcasted_iota(
        jnp.int32, (LANE, LANE), 1
    )
    copies_in[0].wait()
    for b in range(NORB // LANE):
        part = slice(b * LANE, (b + 1) * LANE)
        tile = jnp.where(eye, g_v[1, part, part].astype(F32), 0.0)
        zbuf[0, b : b + 1, :] = jnp.sum(tile, axis=0, keepdims=True)
    zbuf[0, 8:16, :] = great[...]

    def ring_copy(d):
        return pltpu.make_async_remote_copy(
            zbuf.at[0], zbuf.at[d], zs.at[d], zr.at[d],
            device_id=ring_mate(d), device_id_type=MESH,
        )

    for d in range(1, RING):
        ring_copy(d).start()

    for c in range(2):

        @pl.loop(0, NORB // BLOCK)
        def _(i):
            acc[c, pl.ds(i * BLOCK, BLOCK), :] = jnp.zeros((BLOCK, NORB), F32)

    copies_in[1].wait()
    copies_in[2].wait()
    weight_copy.wait()
    m_low, m_high = wrecv[0, 0:1, 0:1], wrecv[1, 0:1, 0:1]

    def plane_copy(t):
        return pltpu.make_async_remote_copy(
            pbuf.at[t], qbuf.at[t], ps.at[t], pr.at[t],
            device_id=plane_mate(t), device_id_type=MESH,
        )

    def partial_sums():
        for d in range(1, RING):
            ring_copy(d).wait()

        @pl.loop(0, RING)
        def _(t):
            row = (((y + t // 2) % LAYERS) * RING + z) * 2 + (h + t % 2) % 2
            less = jnp.zeros((8, LANE), F32)
            more = jnp.zeros((8, LANE), F32)
            for d in range(RING):
                column = (y * RING + (z - d + RING) % RING) * 2 + h
                k_less = jnp.float32(0.0)
                k_great = jnp.float32(0.0)
                for m in range(MODES):
                    up = column - row == lags[m]
                    down = row - column == lags[m]
                    first, second = strengths[0, m], strengths[1, m]
                    k_less += jnp.where(up, first, 0.0) + jnp.where(down, second, 0.0)
                    k_great += jnp.where(up, second, 0.0) + jnp.where(down, first, 0.0)
                less += k_less * zbuf[d, 0:8, :]
                more += k_great * zbuf[d, 8:16, :]
            pbuf[t, 0:8, :] = less
            pbuf[t, 8:16, :] = more

        for t in range(1, RING):
            plane_copy(t).start()

    def neighbour_copy(side):
        return pltpu.make_async_remote_copy(
            nsend.at[side], nbuf.at[side], ns.at[side], nr.at[side],
            device_id=(e, s + 1 - 2 * side), device_id_type=MESH,
        )

    goes_up, goes_down = s + 1 < SLABS, s > 0

    def correlate():
        total = pbuf[0]
        for t in range(1, RING):
            plane_copy(t).wait()
            total += qbuf[t]
        nsend[1] = total
        for part in (slice(0, 8), slice(8, 16)):
            nsend[0, part, :] = coupling[...] * total[part, :]

        @pl.when(goes_up)
        def _():
            neighbour_copy(0).start()

        @pl.when(goes_down)
        def _():
            neighbour_copy(1).start()

        @pl.when(jnp.logical_not(goes_down))
        def _():
            nbuf[0] = jnp.zeros((16, LANE), F32)

        @pl.when(jnp.logical_not(goes_up))
        def _():
            nbuf[1] = jnp.zeros((16, LANE), F32)

    def couple():
        @pl.when(goes_up)
        def _():
            neighbour_copy(0).wait_send()
            neighbour_copy(1).wait_recv()

        @pl.when(goes_down)
        def _():
            neighbour_copy(1).wait_send()
            neighbour_copy(0).wait_recv()

        for part in (slice(0, 8), slice(8, 16)):
            phon[part, :] = nsend[1, part, :] + nbuf[0, part, :] + coupling[...] * nbuf[1, part, :]
        great_out[...] = phon[8:16, :]

    def multiply(c, k, mixed):
        left[c] = lax.dot_general(
            mixed, d_v[...], (((1,), (1,)), ((), ())), preferred_element_type=F32
        ).astype(BF16)
        columns = pl.ds(pl.multiple_of(k * ROWS, ROWS), ROWS)

        @pl.loop(0, NORB // BLOCK)
        def _(i):
            rows = pl.ds(pl.multiple_of(i * BLOCK, BLOCK), BLOCK)
            acc[c, rows, :] += jnp.dot(d_v[rows, columns], left[c], preferred_element_type=F32)

    def own(c, k):
        return own_w * g_v[c, pl.ds(k * ROWS, ROWS), :].astype(F32)

    @pl.loop(0, CHUNKS + LAG)
    def _(k):
        @pl.when(k < CHUNKS)
        def _():
            arrive(CROSS, k)
            start(LOW, k)
            start(HIGH, k)
            arrive(BLOW, k)
            arrive(BHIGH, k)
            sums_out[k] = (m_low * blow[k].astype(F32) + m_high * bhigh[k].astype(F32)).astype(BF16)
            start(SUMS, k)

        @pl.when(k == 2)
        def _():
            partial_sums()

        @pl.when(k == 4)
        def _():
            correlate()

        @pl.when(k == 6)
        def _():
            couple()

        @pl.when(k >= LAG)
        def _():
            j = k - LAG
            arrive(SUMS, j)
            multiply(1, j, (own(1, j) + sums[j].astype(F32)).astype(BF16))

    def write(c):
        return pltpu.make_async_copy(stage.at[c], out.at[c], osem.at[c])

    def finish(c):
        for i in range(NORB // LANE):
            rows = slice(i * LANE, (i + 1) * LANE)
            stage[c, rows, :] = acc[c, rows, :].astype(BF16)
            if c == 1:
                stage[1, rows, rows] = (
                    acc[1, rows, rows] + jnp.where(eye, phon[i : i + 1, :], 0.0)
                ).astype(BF16)
        write(c).start()

    finish(1)

    @pl.loop(0, CHUNKS)
    def _(k):
        arrive(LOW, k)
        arrive(HIGH, k)
        mixed = own(0, k) + low_w * low[k].astype(F32) + high_w * high[k].astype(F32)
        multiply(0, k, mixed.astype(BF16))

    finish(0)

    @pl.loop(0, CHUNKS)
    def _(k):
        for stream in (CROSS, LOW, HIGH, BLOW, BHIGH, SUMS):
            sent(stream, k)

    write(1).wait()
    write(0).wait()


def on_device(lesser, great, dipole, weights, flags, lags, strengths, coupling):
    vmem = pl.BlockSpec(memory_space=pltpu.VMEM)
    smem = pl.BlockSpec(memory_space=pltpu.SMEM)
    hbm = pl.BlockSpec(memory_space=pl.ANY)
    chunks = pltpu.VMEM((CHUNKS, ROWS, NORB), BF16)
    dma = pltpu.SemaphoreType.DMA
    out, great_out = pl.pallas_call(
        body,
        out_shape=(
            jax.ShapeDtypeStruct((2, NORB, NORB), BF16),
            jax.ShapeDtypeStruct((8, LANE), F32),
        ),
        in_specs=[hbm, vmem, hbm, smem, smem, smem, smem, vmem],
        out_specs=(hbm, vmem),
        scratch_shapes=[
            pltpu.VMEM((2, NORB, NORB), BF16),
            pltpu.VMEM((NORB, NORB), BF16),
            chunks, chunks, chunks, chunks, chunks, chunks, chunks,
            pltpu.VMEM((2, ROWS, NORB), BF16),
            pltpu.VMEM((2, NORB, NORB), F32),
            pltpu.VMEM((2, NORB, NORB), BF16),
            pltpu.VMEM((RING, 16, LANE), F32),
            pltpu.VMEM((RING, 16, LANE), F32),
            pltpu.VMEM((RING, 16, LANE), F32),
            pltpu.VMEM((2, 16, LANE), F32),
            pltpu.VMEM((2, 16, LANE), F32),
            pltpu.VMEM((16, LANE), F32),
            pltpu.VMEM((2, 8, LANE), F32),
            pltpu.VMEM((2, 8, LANE), F32),
            dma((6, CHUNKS)), dma((6, CHUNKS)),
            dma((RING,)), dma((RING,)),
            dma((RING,)), dma((RING,)),
            dma((2,)), dma((2,)),
            dma, dma,
            dma((3,)), dma((2,)),
        ],
        name="stencil",
        cost_estimate=pl.CostEstimate(
            flops=8 * NORB**3, bytes_accessed=10 * NORB * NORB, transcendentals=0
        ),
        compiler_params=pltpu.CompilerParams(
            collective_id=0, has_side_effects=True, vmem_limit_bytes=56 << 20
        ),
    )(
        lesser.reshape(2, NORB, NORB), great.reshape(8, LANE), dipole.reshape(NORB, NORB),
        weights, flags, lags, strengths, coupling.reshape(8, LANE),
    )
    return out.reshape(1, 1, 2, NORB, NORB), great_out.reshape(1, 1, NORB)


def solution(mesh):
    return jax.shard_map(
        on_device,
        mesh=mesh,
        in_specs=(
            P("energy", "slab", None, None, None),
            P("energy", "slab", None),
            P("slab", None, None),
            P("energy", None),
            P("energy"),
            P(),
            P(),
            P("slab", None),
        ),
        out_specs=(P("energy", "slab", None, None, None), P("energy", "slab", None)),
        check_vma=False,
    )
```

```python
import jax
import jax.numpy as jnp
from jax import lax
from jax.experimental import pallas as pl
from jax.experimental.pallas import tpu as pltpu
from jax.sharding import PartitionSpec as P

F32, BF16 = jnp.float32, jnp.bfloat16
MESH = pl.DeviceIdType.MESH

RING = 8
LAYERS = 4
CHAIN = RING * LAYERS
SLABS = 4
MODES = 6
NORB = 1024
ROWS = 128
CHUNKS = NORB // ROWS
TILE = 128
PER = TILE // ROWS
AHEAD = 3
LAG_SUM = 1
LAG_OWN = 3
STAGES = (2, 3, 4)
BLOCK = 256
LANE = 128

CROSS, LOW, HIGH, BLOW, BHIGH, SUMS = range(6)


def body(
    lesser, great, dip, weights, flags, lags, strengths, coupling,
    out, great_out,
    g_v, d_v, d_t, crossed, low, high, blow, bhigh, sums, sums_out, left, acc,
    diagonal, zbuf, pbuf, qbuf, nbuf, nsend, phon, wsend, wrecv,
    send, recv, zs, zr, ps, pr, ns, nr, ws, wr, local,
):
    e = lax.axis_index("energy")
    s = lax.axis_index("slab")
    w, h = e // 2, e % 2
    y, z = w // RING, w % RING
    mirror = (w * 2 + (1 - h), s)

    def at(chain):
        return (chain * 2 + h, s)

    def inside(chain):
        return jnp.logical_and(chain >= 0, chain < CHAIN)

    a_low, a_high = h - 2, h + 1
    b_low, b_high = -1 - h, 2 - h

    copies_in = [
        pltpu.make_async_copy(lesser.at[1], g_v.at[1], local.at[0]),
        pltpu.make_async_copy(lesser.at[0], g_v.at[0], local.at[1]),
        pltpu.make_async_copy(dip, d_v, local.at[2]),
    ]
    for copy in copies_in:
        copy.start()

    barrier = pltpu.get_barrier_semaphore()
    expected = jnp.int32(2 * (RING - 1))
    for step in (-2, -1, 1, 2):
        ok = inside(w + step)
        expected = expected + ok.astype(jnp.int32)

        @pl.when(ok)
        def _():
            pl.semaphore_signal(barrier, inc=1, device_id=at(w + step), device_id_type=MESH)

    def ring_mate(d):
        return ((y * RING + (z + d) % RING) * 2 + h, s)

    def plane_mate(t):
        return ((((y + t // 2) % LAYERS) * RING + z) * 2 + (h + t % 2) % 2, s)

    for d in range(1, RING):
        pl.semaphore_signal(barrier, inc=1, device_id=ring_mate(d), device_id_type=MESH)
        pl.semaphore_signal(barrier, inc=1, device_id=plane_mate(d), device_id_type=MESH)
    for step in (-1, 1):
        ok = jnp.logical_and(s + step >= 0, s + step < SLABS)
        expected = expected + ok.astype(jnp.int32)

        @pl.when(ok)
        def _():
            pl.semaphore_signal(barrier, inc=1, device_id=(e, s + step), device_id_type=MESH)

    pl.semaphore_wait(barrier, expected)

    def chunk_copy(stream, k):
        rows = pl.ds(pl.multiple_of(k * ROWS, ROWS), ROWS)
        source, target, device = {
            CROSS: (lesser.at[0, rows], crossed.at[rows], mirror),
            LOW: (crossed.at[rows], low.at[rows], at(w - a_low)),
            HIGH: (crossed.at[rows], high.at[rows], at(w - a_high)),
            BLOW: (lesser.at[1, rows], blow.at[rows], at(w - b_low)),
            BHIGH: (lesser.at[1, rows], bhigh.at[rows], at(w - b_high)),
            SUMS: (sums_out.at[rows], sums.at[rows], mirror),
        }[stream]
        return pltpu.make_async_remote_copy(
            source, target, send.at[stream, k], recv.at[stream, k],
            device_id=device, device_id_type=MESH,
        )

    sends_to = {
        LOW: inside(w - a_low), HIGH: inside(w - a_high),
        BLOW: inside(w - b_low), BHIGH: inside(w - b_high),
    }
    hears = {
        LOW: inside(w + a_low), HIGH: inside(w + a_high),
        BLOW: inside(w + b_low), BHIGH: inside(w + b_high),
    }

    def start(stream, k):
        if stream in sends_to:

            @pl.when(sends_to[stream])
            def _():
                chunk_copy(stream, k).start()
        else:
            chunk_copy(stream, k).start()

    def arrive(stream, k):
        if stream in hears:

            @pl.when(hears[stream])
            def _():
                chunk_copy(stream, k).wait_recv()
        else:
            chunk_copy(stream, k).wait_recv()

    def sent(stream, k):
        if stream in sends_to:

            @pl.when(sends_to[stream])
            def _():
                chunk_copy(stream, k).wait_send()
        else:
            chunk_copy(stream, k).wait_send()

    flag = flags[0].astype(F32)
    own_w, low_w, high_w = weights[0, 0], flag * weights[0, 1], flag * weights[0, 2]
    wsend[0] = jnp.full((8, LANE), low_w, F32)
    wsend[1] = jnp.full((8, LANE), high_w, F32)
    weight_copy = pltpu.make_async_remote_copy(
        wsend, wrecv, ws, wr, device_id=mirror, device_id_type=MESH
    )
    weight_copy.start()

    @pl.loop(0, AHEAD)
    def _(k):
        start(CROSS, k)
        start(BHIGH, k)
        start(BLOW, k)

    for stream, buffer in ((LOW, low), (HIGH, high), (BLOW, blow), (BHIGH, bhigh)):

        @pl.when(jnp.logical_not(hears[stream]))
        def _():
            @pl.loop(0, NORB // TILE)
            def _(k):
                buffer[pl.ds(pl.multiple_of(k * TILE, TILE), TILE)] = jnp.zeros((TILE, NORB), BF16)

    eye = lax.broadcasted_iota(jnp.int32, (LANE, LANE), 0) == lax.broadcasted_iota(
        jnp.int32, (LANE, LANE), 1
    )
    copies_in[0].wait()
    for b in range(NORB // LANE):
        part = slice(b * LANE, (b + 1) * LANE)
        tile = jnp.where(eye, g_v[1, part, part].astype(F32), 0.0)
        diagonal[b : b + 1, :] = jnp.sum(tile, axis=0, keepdims=True)
    diagonal[8:16, :] = great[...]
    zbuf[0] = diagonal[...].astype(BF16)

    def ring_copy(d):
        return pltpu.make_async_remote_copy(
            zbuf.at[0], zbuf.at[d], zs.at[d], zr.at[d],
            device_id=ring_mate(d), device_id_type=MESH,
        )

    for d in range(1, RING):
        ring_copy(d).start()

    for c in range(2):

        @pl.loop(0, NORB // BLOCK)
        def _(i):
            acc[c, pl.ds(i * BLOCK, BLOCK), :] = jnp.zeros((BLOCK, NORB), F32)

    copies_in[1].wait()
    copies_in[2].wait()

    @pl.loop(0, NORB // LANE)
    def _(i):
        part = pl.ds(pl.multiple_of(i * LANE, LANE), LANE)
        d_t[:, part] = d_v[part, :].T

    weight_copy.wait()
    m_low, m_high = wrecv[0, 0:1, 0:1], wrecv[1, 0:1, 0:1]

    def plane_copy(t):
        return pltpu.make_async_remote_copy(
            pbuf.at[t], qbuf.at[t], ps.at[t], pr.at[t],
            device_id=plane_mate(t), device_id_type=MESH,
        )

    def partial_sums():
        for d in range(1, RING):
            ring_copy(d).wait()

        @pl.loop(0, RING)
        def _(t):
            row = (((y + t // 2) % LAYERS) * RING + z) * 2 + (h + t % 2) % 2
            less = jnp.zeros((8, LANE), F32)
            more = jnp.zeros((8, LANE), F32)
            for d in range(RING):
                column = (y * RING + (z - d + RING) % RING) * 2 + h
                k_less = jnp.float32(0.0)
                k_great = jnp.float32(0.0)
                for m in range(MODES):
                    up = column - row == lags[m]
                    down = row - column == lags[m]
                    first, second = strengths[0, m], strengths[1, m]
                    k_less += jnp.where(up, first, 0.0) + jnp.where(down, second, 0.0)
                    k_great += jnp.where(up, second, 0.0) + jnp.where(down, first, 0.0)
                held = diagonal[...] if d == 0 else zbuf[d].astype(F32)
                less += k_less * held[0:8]
                more += k_great * held[8:16]
            pbuf[t, 0:8, :] = less
            pbuf[t, 8:16, :] = more

        for t in range(1, RING):
            plane_copy(t).start()

    def neighbour_copy(side):
        return pltpu.make_async_remote_copy(
            nsend.at[side], nbuf.at[side], ns.at[side], nr.at[side],
            device_id=(e, s + 1 - 2 * side), device_id_type=MESH,
        )

    goes_up, goes_down = s + 1 < SLABS, s > 0

    def correlate():
        total = pbuf[0]
        for t in range(1, RING):
            plane_copy(t).wait()
            total += qbuf[t]
        nsend[1] = total
        for part in (slice(0, 8), slice(8, 16)):
            nsend[0, part, :] = coupling[...] * total[part, :]

        @pl.when(goes_up)
        def _():
            neighbour_copy(0).start()

        @pl.when(goes_down)
        def _():
            neighbour_copy(1).start()

        @pl.when(jnp.logical_not(goes_down))
        def _():
            nbuf[0] = jnp.zeros((16, LANE), F32)

        @pl.when(jnp.logical_not(goes_up))
        def _():
            nbuf[1] = jnp.zeros((16, LANE), F32)

    def couple():
        @pl.when(goes_up)
        def _():
            neighbour_copy(0).wait_send()
            neighbour_copy(1).wait_recv()

        @pl.when(goes_down)
        def _():
            neighbour_copy(1).wait_send()
            neighbour_copy(0).wait_recv()

        for part in (slice(0, 8), slice(8, 16)):
            phon[part, :] = nsend[1, part, :] + nbuf[0, part, :] + coupling[...] * nbuf[1, part, :]
        great_out[...] = phon[8:16, :]

    def multiply(c, tile, mixed, last):
        left[c] = jnp.dot(mixed, d_t[...], preferred_element_type=F32).astype(BF16)
        if not last:

            @pl.loop(0, NORB // BLOCK)
            def _(i):
                rows = pl.ds(pl.multiple_of(i * BLOCK, BLOCK), BLOCK)
                acc[c, rows, :] += jnp.dot(d_v[rows, tile], left[c], preferred_element_type=F32)

            return

        @pl.loop(0, NORB // BLOCK)
        def _(i):
            rows = pl.ds(pl.multiple_of(i * BLOCK, BLOCK), BLOCK)
            total = acc[c, rows, :] + jnp.dot(
                d_v[rows, tile], left[c], preferred_element_type=F32
            )
            if c == 1:
                acc[1, rows, :] = total
            out[c, rows, :] = total.astype(BF16)

        if c == 1:
            for i in range(NORB // LANE):
                rows = slice(i * LANE, (i + 1) * LANE)
                out[1, rows, rows] = (
                    acc[1, rows, rows] + jnp.where(eye, phon[i : i + 1, :], 0.0)
                ).astype(BF16)

    def with_sums(group, last=False):
        for i in range(PER):
            arrive(SUMS, group * PER + i)
        tile = pl.ds(pl.multiple_of(group * TILE, TILE), TILE)
        mixed = own_w * g_v[1, tile].astype(F32) + sums[tile].astype(F32)
        multiply(1, tile, mixed.astype(BF16), last)

    def with_sides(group, last=False):
        for i in range(PER):
            arrive(LOW, group * PER + i)
            arrive(HIGH, group * PER + i)
        tile = pl.ds(pl.multiple_of(group * TILE, TILE), TILE)
        mixed = (
            own_w * g_v[0, tile].astype(F32)
            + low_w * low[tile].astype(F32)
            + high_w * high[tile].astype(F32)
        )
        multiply(0, tile, mixed.astype(BF16), last)

    @pl.loop(0, CHUNKS)
    def _(k):
        arrive(CROSS, k)
        start(HIGH, k)
        start(LOW, k)

        @pl.when(k + AHEAD < CHUNKS)
        def _():
            start(CROSS, k + AHEAD)

        arrive(BLOW, k)
        arrive(BHIGH, k)

        @pl.when(k + AHEAD < CHUNKS)
        def _():
            start(BHIGH, k + AHEAD)
            start(BLOW, k + AHEAD)

        rows = pl.ds(pl.multiple_of(k * ROWS, ROWS), ROWS)
        sums_out[rows] = (
            m_low * blow[rows].astype(F32) + m_high * bhigh[rows].astype(F32)
        ).astype(BF16)
        start(SUMS, k)

        for stage_at, action in zip(STAGES, (partial_sums, correlate, couple)):

            @pl.when(k == stage_at)
            def _():
                action()

        j = k - LAG_SUM

        @pl.when(jnp.logical_and(j >= 0, j % PER == PER - 1))
        def _():
            with_sums(j // PER)

        i = k - LAG_OWN

        @pl.when(jnp.logical_and(i >= 0, i % PER == PER - 1))
        def _():
            with_sides(i // PER)

    groups = CHUNKS // PER
    for group in range((CHUNKS - LAG_SUM) // PER, groups):
        with_sums(group, group == groups - 1)
    for group in range((CHUNKS - LAG_OWN) // PER, groups):
        with_sides(group, group == groups - 1)

    @pl.loop(0, CHUNKS)
    def _(k):
        for stream in (CROSS, LOW, HIGH, BLOW, BHIGH, SUMS):
            sent(stream, k)


def store(result, great_result, out, great_out, sems):
    copies = [
        pltpu.make_async_copy(result, out, sems.at[0]),
        pltpu.make_async_copy(great_result, great_out, sems.at[1]),
    ]
    for copy in copies:
        copy.start()
    for copy in copies:
        copy.wait()


def in_hbm(x):
    return pltpu.with_memory_space_constraint(x, pltpu.HBM)


def on_device(lesser, great, dipole, weights, flags, lags, strengths, coupling):
    vmem = pl.BlockSpec(memory_space=pltpu.VMEM)
    smem = pl.BlockSpec(memory_space=pltpu.SMEM)
    hbm = pl.BlockSpec(memory_space=pltpu.HBM)
    chunks = pltpu.VMEM((NORB, NORB), BF16)
    dma = pltpu.SemaphoreType.DMA
    result, great_result = pl.pallas_call(
        body,
        out_shape=(
            pltpu.VMEM((2, NORB, NORB), BF16),
            pltpu.VMEM((8, LANE), F32),
        ),
        in_specs=[hbm, vmem, hbm, smem, smem, smem, smem, vmem],
        out_specs=(vmem, vmem),
        scratch_shapes=[
            pltpu.VMEM((2, NORB, NORB), BF16),
            pltpu.VMEM((NORB, NORB), BF16),
            pltpu.VMEM((NORB, NORB), BF16),
            chunks, chunks, chunks, chunks, chunks, chunks, chunks,
            pltpu.VMEM((2, TILE, NORB), BF16),
            pltpu.VMEM((2, NORB, NORB), F32),
            pltpu.VMEM((16, LANE), F32),
            pltpu.VMEM((RING, 16, LANE), BF16),
            pltpu.VMEM((RING, 16, LANE), F32),
            pltpu.VMEM((RING, 16, LANE), F32),
            pltpu.VMEM((2, 16, LANE), F32),
            pltpu.VMEM((2, 16, LANE), F32),
            pltpu.VMEM((16, LANE), F32),
            pltpu.VMEM((2, 8, LANE), F32),
            pltpu.VMEM((2, 8, LANE), F32),
            dma((6, CHUNKS)), dma((6, CHUNKS)),
            dma((RING,)), dma((RING,)),
            dma((RING,)), dma((RING,)),
            dma((2,)), dma((2,)),
            dma, dma,
            dma((3,)),
        ],
        name="stencil",
        cost_estimate=pl.CostEstimate(
            flops=8 * NORB**3, bytes_accessed=10 * NORB * NORB, transcendentals=0
        ),
        compiler_params=pltpu.CompilerParams(
            collective_id=0, has_side_effects=True, vmem_limit_bytes=40 << 20
        ),
    )(
        in_hbm(lesser.reshape(2, NORB, NORB)), in_hbm(great.reshape(8, LANE)),
        in_hbm(dipole.reshape(NORB, NORB)), in_hbm(weights), flags, in_hbm(lags),
        in_hbm(strengths), in_hbm(coupling.reshape(8, LANE)),
    )
    out, great_out = pl.pallas_call(
        store,
        out_shape=(
            jax.ShapeDtypeStruct((2, NORB, NORB), BF16),
            jax.ShapeDtypeStruct((8, LANE), F32),
        ),
        in_specs=[vmem, vmem],
        out_specs=(hbm, hbm),
        scratch_shapes=[dma((2,))],
        name="store",
        compiler_params=pltpu.CompilerParams(vmem_limit_bytes=8 << 20),
    )(result, great_result)
    return out.reshape(1, 1, 2, NORB, NORB), great_out.reshape(1, 1, NORB)


def solution(mesh):
    return jax.shard_map(
        on_device,
        mesh=mesh,
        in_specs=(
            P("energy", "slab", None, None, None),
            P("energy", "slab", None),
            P("slab", None, None),
            P("energy", None),
            P("energy"),
            P(),
            P(),
            P("slab", None),
        ),
        out_specs=(P("energy", "slab", None, None, None), P("energy", "slab", None)),
        check_vma=False,
    )
```

```python
import jax
import jax.numpy as jnp
from jax import lax
from jax.experimental import pallas as pl
from jax.experimental.pallas import tpu as pltpu
from jax.sharding import PartitionSpec as P

F32, BF16 = jnp.float32, jnp.bfloat16
MESH = pl.DeviceIdType.MESH

RING = 8
LAYERS = 4
CHAIN = RING * LAYERS
SLABS = 4
MODES = 6
NORB = 1024
ROWS = 128
CHUNKS = NORB // ROWS
TILE = 128
PER = TILE // ROWS
AHEAD = 4
LAG_SUM = 1
LAG_OWN = 4
STAGES = (3, 4, 5)
BLOCK = 256
LANE = 128

CROSS, LOW, HIGH, BLOW, BHIGH, SUMS = range(6)


def body(
    lesser, great_in, dip, weights_in, flags, lags_in, strengths_in, coupling_in,
    total_real, left_last, d_last, out_imag, great_out,
    great, coupling, weights, lags, strengths, g_v, d_v, d_t, crossed, low, high, blow, bhigh, sums, sums_out, left, total_imag,
    diagonal, zbuf, pbuf, qbuf, nbuf, nsend, phon, wsend, wrecv,
    send, recv, zs, zr, ps, pr, ns, nr, ws, wr, local,
):
    e = lax.axis_index("energy")
    s = lax.axis_index("slab")
    w, h = e // 2, e % 2
    y, z = w // RING, w % RING
    mirror = (w * 2 + (1 - h), s)

    def at(chain):
        return (chain * 2 + h, s)

    def inside(chain):
        return jnp.logical_and(chain >= 0, chain < CHAIN)

    a_low, a_high = h - 2, h + 1
    b_low, b_high = -1 - h, 2 - h

    pairs = (
        (weights_in, weights), (great_in, great), (lesser.at[1], g_v.at[1]),
        (lags_in, lags), (strengths_in, strengths), (coupling_in, coupling),
        (lesser.at[0], g_v.at[0]), (dip, d_v),
    )
    copies_in = [pltpu.make_async_copy(*pair, local.at[i]) for i, pair in enumerate(pairs)]

    barrier = pltpu.get_barrier_semaphore()
    expected = jnp.int32(2 * (RING - 1))
    for step in (-2, -1, 1, 2):
        ok = inside(w + step)
        expected = expected + ok.astype(jnp.int32)

        @pl.when(ok)
        def _():
            pl.semaphore_signal(barrier, inc=1, device_id=at(w + step), device_id_type=MESH)

    def ring_mate(d):
        return ((y * RING + (z + d) % RING) * 2 + h, s)

    def plane_mate(t):
        return ((((y + t // 2) % LAYERS) * RING + z) * 2 + (h + t % 2) % 2, s)

    for d in range(1, RING):
        pl.semaphore_signal(barrier, inc=1, device_id=ring_mate(d), device_id_type=MESH)
        pl.semaphore_signal(barrier, inc=1, device_id=plane_mate(d), device_id_type=MESH)
    for step in (-1, 1):
        ok = jnp.logical_and(s + step >= 0, s + step < SLABS)
        expected = expected + ok.astype(jnp.int32)

        @pl.when(ok)
        def _():
            pl.semaphore_signal(barrier, inc=1, device_id=(e, s + step), device_id_type=MESH)

    pl.semaphore_wait(barrier, expected)

    def chunk_copy(stream, k):
        rows = pl.ds(pl.multiple_of(k * ROWS, ROWS), ROWS)
        source, target, device = {
            CROSS: (lesser.at[0, rows], crossed.at[rows], mirror),
            LOW: (crossed.at[rows], low.at[rows], at(w - a_low)),
            HIGH: (crossed.at[rows], high.at[rows], at(w - a_high)),
            BLOW: (lesser.at[1, rows], blow.at[rows], at(w - b_low)),
            BHIGH: (lesser.at[1, rows], bhigh.at[rows], at(w - b_high)),
            SUMS: (sums_out.at[rows], sums.at[rows], mirror),
        }[stream]
        return pltpu.make_async_remote_copy(
            source, target, send.at[stream, k], recv.at[stream, k],
            device_id=device, device_id_type=MESH,
        )

    sends_to = {
        LOW: inside(w - a_low), HIGH: inside(w - a_high),
        BLOW: inside(w - b_low), BHIGH: inside(w - b_high),
    }
    hears = {
        LOW: inside(w + a_low), HIGH: inside(w + a_high),
        BLOW: inside(w + b_low), BHIGH: inside(w + b_high),
    }

    def start(stream, k):
        if stream in sends_to:

            @pl.when(sends_to[stream])
            def _():
                chunk_copy(stream, k).start()
        else:
            chunk_copy(stream, k).start()

    def arrive(stream, k):
        if stream in hears:

            @pl.when(hears[stream])
            def _():
                chunk_copy(stream, k).wait_recv()
        else:
            chunk_copy(stream, k).wait_recv()

    def sent(stream, k):
        if stream in sends_to:

            @pl.when(sends_to[stream])
            def _():
                chunk_copy(stream, k).wait_send()
        else:
            chunk_copy(stream, k).wait_send()

    @pl.loop(0, AHEAD)
    def _(k):
        start(CROSS, k)
        start(BHIGH, k)
        start(BLOW, k)

    for copy in copies_in:
        copy.start()
    for copy in copies_in[:3]:
        copy.wait()

    flag = flags[0].astype(F32)
    own_w, low_w, high_w = weights[0, 0], flag * weights[0, 1], flag * weights[0, 2]
    wsend[0] = jnp.full((8, LANE), low_w, F32)
    wsend[1] = jnp.full((8, LANE), high_w, F32)
    weight_copy = pltpu.make_async_remote_copy(
        wsend, wrecv, ws, wr, device_id=mirror, device_id_type=MESH
    )
    weight_copy.start()

    for stream, buffer in ((LOW, low), (HIGH, high), (BLOW, blow), (BHIGH, bhigh)):

        @pl.when(jnp.logical_not(hears[stream]))
        def _():
            @pl.loop(0, NORB // TILE)
            def _(k):
                buffer[pl.ds(pl.multiple_of(k * TILE, TILE), TILE)] = jnp.zeros((TILE, NORB), BF16)

    eye = lax.broadcasted_iota(jnp.int32, (LANE, LANE), 0) == lax.broadcasted_iota(
        jnp.int32, (LANE, LANE), 1
    )
    for b in range(NORB // LANE):
        part = slice(b * LANE, (b + 1) * LANE)
        tile = jnp.where(eye, g_v[1, part, part].astype(F32), 0.0)
        diagonal[b : b + 1, :] = jnp.sum(tile, axis=0, keepdims=True)
    diagonal[8:16, :] = great[...]
    zbuf[0] = diagonal[...].astype(BF16)

    def ring_copy(d):
        return pltpu.make_async_remote_copy(
            zbuf.at[0], zbuf.at[d], zs.at[d], zr.at[d],
            device_id=ring_mate(d), device_id_type=MESH,
        )

    for d in range(1, RING):
        ring_copy(d).start()

    totals = (total_real, total_imag)
    for total in totals:

        @pl.loop(0, NORB // BLOCK)
        def _(i):
            total[pl.ds(i * BLOCK, BLOCK), :] = jnp.zeros((BLOCK, NORB), F32)

    for copy in copies_in[3:]:
        copy.wait()

    @pl.loop(0, NORB // LANE)
    def _(i):
        part = pl.ds(pl.multiple_of(i * LANE, LANE), LANE)
        d_t[:, part] = d_v[part, :].T

    d_last[...] = d_v[:, NORB - TILE :]

    weight_copy.wait()
    m_low, m_high = wrecv[0, 0:1, 0:1], wrecv[1, 0:1, 0:1]

    def plane_copy(t):
        return pltpu.make_async_remote_copy(
            pbuf.at[t], qbuf.at[t], ps.at[t], pr.at[t],
            device_id=plane_mate(t), device_id_type=MESH,
        )

    def partial_sums():
        for d in range(1, RING):
            ring_copy(d).wait()

        @pl.loop(0, RING)
        def _(t):
            row = (((y + t // 2) % LAYERS) * RING + z) * 2 + (h + t % 2) % 2
            less = jnp.zeros((8, LANE), F32)
            more = jnp.zeros((8, LANE), F32)
            for d in range(RING):
                column = (y * RING + (z - d + RING) % RING) * 2 + h
                k_less = jnp.float32(0.0)
                k_great = jnp.float32(0.0)
                for m in range(MODES):
                    up = column - row == lags[m]
                    down = row - column == lags[m]
                    first, second = strengths[0, m], strengths[1, m]
                    k_less += jnp.where(up, first, 0.0) + jnp.where(down, second, 0.0)
                    k_great += jnp.where(up, second, 0.0) + jnp.where(down, first, 0.0)
                held = diagonal[...] if d == 0 else zbuf[d].astype(F32)
                less += k_less * held[0:8]
                more += k_great * held[8:16]
            pbuf[t, 0:8, :] = less
            pbuf[t, 8:16, :] = more

        for t in range(1, RING):
            plane_copy(t).start()

    def neighbour_copy(side):
        return pltpu.make_async_remote_copy(
            nsend.at[side], nbuf.at[side], ns.at[side], nr.at[side],
            device_id=(e, s + 1 - 2 * side), device_id_type=MESH,
        )

    goes_up, goes_down = s + 1 < SLABS, s > 0

    def correlate():
        total = pbuf[0]
        for t in range(1, RING):
            plane_copy(t).wait()
            total += qbuf[t]
        nsend[1] = total
        for part in (slice(0, 8), slice(8, 16)):
            nsend[0, part, :] = coupling[...] * total[part, :]

        @pl.when(goes_up)
        def _():
            neighbour_copy(0).start()

        @pl.when(goes_down)
        def _():
            neighbour_copy(1).start()

        @pl.when(jnp.logical_not(goes_down))
        def _():
            nbuf[0] = jnp.zeros((16, LANE), F32)

        @pl.when(jnp.logical_not(goes_up))
        def _():
            nbuf[1] = jnp.zeros((16, LANE), F32)

    def couple():
        @pl.when(goes_up)
        def _():
            neighbour_copy(0).wait_send()
            neighbour_copy(1).wait_recv()

        @pl.when(goes_down)
        def _():
            neighbour_copy(1).wait_send()
            neighbour_copy(0).wait_recv()

        for part in (slice(0, 8), slice(8, 16)):
            phon[part, :] = nsend[1, part, :] + nbuf[0, part, :] + coupling[...] * nbuf[1, part, :]
        great_out[...] = phon[8:16, :]

    def multiply(c, tile, mixed, last):
        product = jnp.dot(mixed, d_t[...], preferred_element_type=F32).astype(BF16)
        if last and c == 0:
            left_last[...] = product
            return
        left[c] = product

        @pl.loop(0, NORB // BLOCK)
        def _(i):
            rows = pl.ds(pl.multiple_of(i * BLOCK, BLOCK), BLOCK)
            total = totals[c][rows, :] + jnp.dot(
                d_v[rows, tile], left[c], preferred_element_type=F32
            )
            totals[c][rows, :] = total
            if last:
                out_imag[rows, :] = total.astype(BF16)

        if last:
            for i in range(NORB // LANE):
                rows = slice(i * LANE, (i + 1) * LANE)
                out_imag[rows, rows] = (
                    total_imag[rows, rows] + jnp.where(eye, phon[i : i + 1, :], 0.0)
                ).astype(BF16)

    def with_sums(group, last=False):
        for i in range(PER):
            arrive(SUMS, group * PER + i)
        tile = pl.ds(pl.multiple_of(group * TILE, TILE), TILE)
        mixed = own_w * g_v[1, tile].astype(F32) + sums[tile].astype(F32)
        multiply(1, tile, mixed.astype(BF16), last)

    def with_sides(group, last=False):
        for i in range(PER):
            arrive(LOW, group * PER + i)
            arrive(HIGH, group * PER + i)
        tile = pl.ds(pl.multiple_of(group * TILE, TILE), TILE)
        mixed = (
            own_w * g_v[0, tile].astype(F32)
            + low_w * low[tile].astype(F32)
            + high_w * high[tile].astype(F32)
        )
        multiply(0, tile, mixed.astype(BF16), last)

    @pl.loop(0, CHUNKS)
    def _(k):
        arrive(CROSS, k)
        start(HIGH, k)
        start(LOW, k)

        @pl.when(k + AHEAD < CHUNKS)
        def _():
            start(CROSS, k + AHEAD)

        arrive(BLOW, k)
        arrive(BHIGH, k)

        @pl.when(k + AHEAD < CHUNKS)
        def _():
            start(BHIGH, k + AHEAD)
            start(BLOW, k + AHEAD)

        rows = pl.ds(pl.multiple_of(k * ROWS, ROWS), ROWS)
        sums_out[rows] = (
            m_low * blow[rows].astype(F32) + m_high * bhigh[rows].astype(F32)
        ).astype(BF16)
        start(SUMS, k)

        for stage_at, action in zip(STAGES, (partial_sums, correlate, couple)):

            @pl.when(k == stage_at)
            def _():
                action()

        j = k - LAG_SUM

        @pl.when(jnp.logical_and(j >= 0, j % PER == PER - 1))
        def _():
            with_sums(j // PER)

        i = k - LAG_OWN

        @pl.when(jnp.logical_and(i >= 0, i % PER == PER - 1))
        def _():
            with_sides(i // PER)

    groups = CHUNKS // PER
    for group in range((CHUNKS - LAG_SUM) // PER, groups):
        with_sums(group, group == groups - 1)
    for group in range((CHUNKS - LAG_OWN) // PER, groups - 1):
        with_sides(group)

    @pl.loop(0, CHUNKS)
    def _(k):
        for stream in (CROSS, BLOW, BHIGH, SUMS):
            sent(stream, k)

    @pl.loop(0, CHUNKS - PER)
    def _(k):
        for stream in (LOW, HIGH):
            sent(stream, k)

    with_sides(groups - 1, True)
    for k in range(CHUNKS - PER, CHUNKS):
        for stream in (LOW, HIGH):
            sent(stream, k)


def store(total, left, dip, imag, great, out, great_out, stage, sems):
    copies = [pltpu.make_async_copy(great, great_out, sems.at[2, 0])]
    blocks = [slice(i * BLOCK, (i + 1) * BLOCK) for i in range(NORB // BLOCK)]
    for i, rows in enumerate(blocks):
        copies.append(pltpu.make_async_copy(imag.at[rows], out.at[1, rows], sems.at[1, i]))
    for copy in copies:
        copy.start()
    for i, rows in enumerate(blocks):
        stage[rows, :] = (
            total[rows, :] + jnp.dot(dip[rows, :], left[...], preferred_element_type=F32)
        ).astype(BF16)
        copy = pltpu.make_async_copy(stage.at[rows], out.at[0, rows], sems.at[0, i])
        copy.start()
        copies.append(copy)
    for copy in copies:
        copy.wait()


def in_hbm(x):
    return pltpu.with_memory_space_constraint(x, pltpu.HBM)


def on_device(lesser, great, dipole, weights, flags, lags, strengths, coupling):
    vmem = pl.BlockSpec(memory_space=pltpu.VMEM)
    smem = pltpu.SMEM
    hbm = pl.BlockSpec(memory_space=pltpu.HBM)
    chunks = pltpu.VMEM((NORB, NORB), BF16)
    dma = pltpu.SemaphoreType.DMA
    results = pl.pallas_call(
        body,
        out_shape=(
            pltpu.VMEM((NORB, NORB), F32),
            pltpu.VMEM((TILE, NORB), BF16),
            pltpu.VMEM((NORB, TILE), BF16),
            pltpu.VMEM((NORB, NORB), BF16),
            pltpu.VMEM((8, LANE), F32),
        ),
        in_specs=[hbm] * 4 + [pl.BlockSpec(memory_space=smem)] + [hbm] * 3,
        out_specs=(vmem,) * 5,
        scratch_shapes=[
            pltpu.VMEM((8, LANE), F32), pltpu.VMEM((8, LANE), F32),
            smem((1, 3), F32), smem((MODES,), jnp.int32), smem((2, MODES), F32),
            pltpu.VMEM((2, NORB, NORB), BF16),
            pltpu.VMEM((NORB, NORB), BF16),
            pltpu.VMEM((NORB, NORB), BF16),
            chunks, chunks, chunks, chunks, chunks, chunks, chunks,
            pltpu.VMEM((2, TILE, NORB), BF16),
            pltpu.VMEM((NORB, NORB), F32),
            pltpu.VMEM((16, LANE), F32),
            pltpu.VMEM((RING, 16, LANE), BF16),
            pltpu.VMEM((RING, 16, LANE), F32),
            pltpu.VMEM((RING, 16, LANE), F32),
            pltpu.VMEM((2, 16, LANE), F32),
            pltpu.VMEM((2, 16, LANE), F32),
            pltpu.VMEM((16, LANE), F32),
            pltpu.VMEM((2, 8, LANE), F32),
            pltpu.VMEM((2, 8, LANE), F32),
            dma((6, CHUNKS)), dma((6, CHUNKS)),
            dma((RING,)), dma((RING,)),
            dma((RING,)), dma((RING,)),
            dma((2,)), dma((2,)),
            dma, dma,
            dma((8,)),
        ],
        name="stencil",
        cost_estimate=pl.CostEstimate(
            flops=8 * NORB**3, bytes_accessed=10 * NORB * NORB, transcendentals=0
        ),
        compiler_params=pltpu.CompilerParams(
            collective_id=0, has_side_effects=True, vmem_limit_bytes=40 << 20
        ),
    )(
        in_hbm(lesser.reshape(2, NORB, NORB)), in_hbm(great.reshape(8, LANE)),
        in_hbm(dipole.reshape(NORB, NORB)), in_hbm(weights), flags, in_hbm(lags),
        in_hbm(strengths), in_hbm(coupling.reshape(8, LANE)),
    )
    out, great_out = pl.pallas_call(
        store,
        out_shape=(
            jax.ShapeDtypeStruct((2, NORB, NORB), BF16),
            jax.ShapeDtypeStruct((8, LANE), F32),
        ),
        in_specs=[vmem] * 5,
        out_specs=(hbm, hbm),
        scratch_shapes=[pltpu.VMEM((NORB, NORB), BF16), dma((3, NORB // BLOCK))],
        name="store",
        compiler_params=pltpu.CompilerParams(vmem_limit_bytes=8 << 20),
    )(*results)
    return out.reshape(1, 1, 2, NORB, NORB), great_out.reshape(1, 1, NORB)


def solution(mesh):
    return jax.shard_map(
        on_device,
        mesh=mesh,
        in_specs=(
            P("energy", "slab", None, None, None),
            P("energy", "slab", None),
            P("slab", None, None),
            P("energy", None),
            P("energy"),
            P(),
            P(),
            P("slab", None),
        ),
        out_specs=(P("energy", "slab", None, None, None), P("energy", "slab", None)),
        check_vma=False,
    )
```

```python
import jax
import jax.numpy as jnp
from jax import lax
from jax.experimental import pallas as pl
from jax.experimental.pallas import tpu as pltpu
from jax.sharding import PartitionSpec as P

F32, BF16 = jnp.float32, jnp.bfloat16
MESH = pl.DeviceIdType.MESH

RING = 8
LAYERS = 4
CHAIN = RING * LAYERS
SLABS = 4
MODES = 6
NORB = 1024
ROWS = 128
CHUNKS = NORB // ROWS
TILE = 128
PER = TILE // ROWS
AHEAD = 5
LAG_SUM = 1
LAG_OWN = 6
STAGES = (3, 4, 5)
BLOCK = 256
LANE = 128

CROSS, LOW, HIGH, BLOW, BHIGH, SUMS = range(6)


def body(
    lesser, great_in, dip, weights_in, flags, lags_in, strengths_in, coupling_in,
    total_real, mixed_last, d_t, d_last, out_imag, great_out,
    great, coupling, weights, lags, strengths, g_v, d_v, crossed, low, high, blow, bhigh, sums, sums_out, left, total_imag,
    diagonal, zbuf, pbuf, qbuf, nbuf, nsend, phon, wsend, wrecv,
    send, recv, zs, zr, ps, pr, ns, nr, ws, wr, local,
):
    e = lax.axis_index("energy")
    s = lax.axis_index("slab")
    w, h = e // 2, e % 2
    y, z = w // RING, w % RING
    mirror = (w * 2 + (1 - h), s)

    def at(chain):
        return (chain * 2 + h, s)

    def inside(chain):
        return jnp.logical_and(chain >= 0, chain < CHAIN)

    a_low, a_high = h - 2, h + 1
    b_low, b_high = -1 - h, 2 - h

    pairs = (
        (weights_in, weights), (great_in, great), (lesser.at[1], g_v.at[1]),
        (lags_in, lags), (strengths_in, strengths), (coupling_in, coupling),
        (lesser.at[0], g_v.at[0]), (dip, d_v),
    )
    copies_in = [pltpu.make_async_copy(*pair, local.at[i]) for i, pair in enumerate(pairs)]

    barrier = pltpu.get_barrier_semaphore()
    expected = jnp.int32(2 * (RING - 1))
    for step in (-2, -1, 1, 2):
        ok = inside(w + step)
        expected = expected + ok.astype(jnp.int32)

        @pl.when(ok)
        def _():
            pl.semaphore_signal(barrier, inc=1, device_id=at(w + step), device_id_type=MESH)

    def ring_mate(d):
        return ((y * RING + (z + d) % RING) * 2 + h, s)

    def plane_mate(t):
        return ((((y + t // 2) % LAYERS) * RING + z) * 2 + (h + t % 2) % 2, s)

    for d in range(1, RING):
        pl.semaphore_signal(barrier, inc=1, device_id=ring_mate(d), device_id_type=MESH)
        pl.semaphore_signal(barrier, inc=1, device_id=plane_mate(d), device_id_type=MESH)
    for step in (-1, 1):
        ok = jnp.logical_and(s + step >= 0, s + step < SLABS)
        expected = expected + ok.astype(jnp.int32)

        @pl.when(ok)
        def _():
            pl.semaphore_signal(barrier, inc=1, device_id=(e, s + step), device_id_type=MESH)

    pl.semaphore_wait(barrier, expected)

    def chunk_copy(stream, k):
        rows = pl.ds(pl.multiple_of(k * ROWS, ROWS), ROWS)
        source, target, device = {
            CROSS: (lesser.at[0, rows], crossed.at[rows], mirror),
            LOW: (crossed.at[rows], low.at[rows], at(w - a_low)),
            HIGH: (crossed.at[rows], high.at[rows], at(w - a_high)),
            BLOW: (lesser.at[1, rows], blow.at[rows], at(w - b_low)),
            BHIGH: (lesser.at[1, rows], bhigh.at[rows], at(w - b_high)),
            SUMS: (sums_out.at[rows], sums.at[rows], mirror),
        }[stream]
        return pltpu.make_async_remote_copy(
            source, target, send.at[stream, k], recv.at[stream, k],
            device_id=device, device_id_type=MESH,
        )

    sends_to = {
        LOW: inside(w - a_low), HIGH: inside(w - a_high),
        BLOW: inside(w - b_low), BHIGH: inside(w - b_high),
    }
    hears = {
        LOW: inside(w + a_low), HIGH: inside(w + a_high),
        BLOW: inside(w + b_low), BHIGH: inside(w + b_high),
    }

    def start(stream, k):
        if stream in sends_to:

            @pl.when(sends_to[stream])
            def _():
                chunk_copy(stream, k).start()
        else:
            chunk_copy(stream, k).start()

    def arrive(stream, k):
        if stream in hears:

            @pl.when(hears[stream])
            def _():
                chunk_copy(stream, k).wait_recv()
        else:
            chunk_copy(stream, k).wait_recv()

    def sent(stream, k):
        if stream in sends_to:

            @pl.when(sends_to[stream])
            def _():
                chunk_copy(stream, k).wait_send()
        else:
            chunk_copy(stream, k).wait_send()

    @pl.loop(0, AHEAD)
    def _(k):
        start(CROSS, k)
        start(BHIGH, k)
        start(BLOW, k)

    for copy in copies_in:
        copy.start()
    for copy in copies_in[:3]:
        copy.wait()

    flag = flags[0].astype(F32)
    own_w, low_w, high_w = weights[0, 0], flag * weights[0, 1], flag * weights[0, 2]
    wsend[0] = jnp.full((8, LANE), low_w, F32)
    wsend[1] = jnp.full((8, LANE), high_w, F32)
    weight_copy = pltpu.make_async_remote_copy(
        wsend, wrecv, ws, wr, device_id=mirror, device_id_type=MESH
    )
    weight_copy.start()

    for stream, buffer in ((LOW, low), (HIGH, high), (BLOW, blow), (BHIGH, bhigh)):

        @pl.when(jnp.logical_not(hears[stream]))
        def _():
            @pl.loop(0, NORB // TILE)
            def _(k):
                buffer[pl.ds(pl.multiple_of(k * TILE, TILE), TILE)] = jnp.zeros((TILE, NORB), BF16)

    eye = lax.broadcasted_iota(jnp.int32, (LANE, LANE), 0) == lax.broadcasted_iota(
        jnp.int32, (LANE, LANE), 1
    )
    for b in range(NORB // LANE):
        part = slice(b * LANE, (b + 1) * LANE)
        tile = jnp.where(eye, g_v[1, part, part].astype(F32), 0.0)
        diagonal[b : b + 1, :] = jnp.sum(tile, axis=0, keepdims=True)
    diagonal[8:16, :] = great[...]
    zbuf[0] = diagonal[...].astype(BF16)

    def ring_copy(d):
        return pltpu.make_async_remote_copy(
            zbuf.at[0], zbuf.at[d], zs.at[d], zr.at[d],
            device_id=ring_mate(d), device_id_type=MESH,
        )

    for d in range(1, RING):
        ring_copy(d).start()

    totals = (total_real, total_imag)
    for total in totals:

        @pl.loop(0, NORB // BLOCK)
        def _(i):
            total[pl.ds(i * BLOCK, BLOCK), :] = jnp.zeros((BLOCK, NORB), F32)

    for copy in copies_in[3:]:
        copy.wait()

    @pl.loop(0, NORB // LANE)
    def _(i):
        part = pl.ds(pl.multiple_of(i * LANE, LANE), LANE)
        d_t[:, part] = d_v[part, :].T

    d_last[...] = d_v[:, NORB - TILE :]

    weight_copy.wait()
    m_low, m_high = wrecv[0, 0:1, 0:1], wrecv[1, 0:1, 0:1]

    def plane_copy(t):
        return pltpu.make_async_remote_copy(
            pbuf.at[t], qbuf.at[t], ps.at[t], pr.at[t],
            device_id=plane_mate(t), device_id_type=MESH,
        )

    def partial_sums():
        for d in range(1, RING):
            ring_copy(d).wait()

        @pl.loop(0, RING)
        def _(t):
            row = (((y + t // 2) % LAYERS) * RING + z) * 2 + (h + t % 2) % 2
            less = jnp.zeros((8, LANE), F32)
            more = jnp.zeros((8, LANE), F32)
            for d in range(RING):
                column = (y * RING + (z - d + RING) % RING) * 2 + h
                k_less = jnp.float32(0.0)
                k_great = jnp.float32(0.0)
                for m in range(MODES):
                    up = column - row == lags[m]
                    down = row - column == lags[m]
                    first, second = strengths[0, m], strengths[1, m]
                    k_less += jnp.where(up, first, 0.0) + jnp.where(down, second, 0.0)
                    k_great += jnp.where(up, second, 0.0) + jnp.where(down, first, 0.0)
                held = diagonal[...] if d == 0 else zbuf[d].astype(F32)
                less += k_less * held[0:8]
                more += k_great * held[8:16]
            pbuf[t, 0:8, :] = less
            pbuf[t, 8:16, :] = more

        for t in range(1, RING):
            plane_copy(t).start()

    def neighbour_copy(side):
        return pltpu.make_async_remote_copy(
            nsend.at[side], nbuf.at[side], ns.at[side], nr.at[side],
            device_id=(e, s + 1 - 2 * side), device_id_type=MESH,
        )

    goes_up, goes_down = s + 1 < SLABS, s > 0

    def correlate():
        total = pbuf[0]
        for t in range(1, RING):
            plane_copy(t).wait()
            total += qbuf[t]
        nsend[1] = total
        for part in (slice(0, 8), slice(8, 16)):
            nsend[0, part, :] = coupling[...] * total[part, :]

        @pl.when(goes_up)
        def _():
            neighbour_copy(0).start()

        @pl.when(goes_down)
        def _():
            neighbour_copy(1).start()

        @pl.when(jnp.logical_not(goes_down))
        def _():
            nbuf[0] = jnp.zeros((16, LANE), F32)

        @pl.when(jnp.logical_not(goes_up))
        def _():
            nbuf[1] = jnp.zeros((16, LANE), F32)

    def couple():
        @pl.when(goes_up)
        def _():
            neighbour_copy(0).wait_send()
            neighbour_copy(1).wait_recv()

        @pl.when(goes_down)
        def _():
            neighbour_copy(1).wait_send()
            neighbour_copy(0).wait_recv()

        for part in (slice(0, 8), slice(8, 16)):
            phon[part, :] = nsend[1, part, :] + nbuf[0, part, :] + coupling[...] * nbuf[1, part, :]
        great_out[...] = phon[8:16, :]

    def multiply(c, tile, mixed, last):
        if last and c == 0:
            mixed_last[...] = mixed
            return
        left[c] = jnp.dot(mixed, d_t[...], preferred_element_type=F32).astype(BF16)

        @pl.loop(0, NORB // BLOCK)
        def _(i):
            rows = pl.ds(pl.multiple_of(i * BLOCK, BLOCK), BLOCK)
            total = totals[c][rows, :] + jnp.dot(
                d_v[rows, tile], left[c], preferred_element_type=F32
            )
            totals[c][rows, :] = total
            if last:
                out_imag[rows, :] = total.astype(BF16)

        if last:
            for i in range(NORB // LANE):
                rows = slice(i * LANE, (i + 1) * LANE)
                out_imag[rows, rows] = (
                    total_imag[rows, rows] + jnp.where(eye, phon[i : i + 1, :], 0.0)
                ).astype(BF16)

    def with_sums(group, last=False):
        for i in range(PER):
            arrive(SUMS, group * PER + i)
        tile = pl.ds(pl.multiple_of(group * TILE, TILE), TILE)
        mixed = own_w * g_v[1, tile].astype(F32) + sums[tile].astype(F32)
        multiply(1, tile, mixed.astype(BF16), last)

    def with_sides(group, last=False):
        for i in range(PER):
            arrive(LOW, group * PER + i)
            arrive(HIGH, group * PER + i)
        tile = pl.ds(pl.multiple_of(group * TILE, TILE), TILE)
        mixed = (
            own_w * g_v[0, tile].astype(F32)
            + low_w * low[tile].astype(F32)
            + high_w * high[tile].astype(F32)
        )
        multiply(0, tile, mixed.astype(BF16), last)

    @pl.loop(0, CHUNKS)
    def _(k):
        arrive(CROSS, k)
        start(HIGH, k)
        start(LOW, k)

        @pl.when(k + AHEAD < CHUNKS)
        def _():
            start(CROSS, k + AHEAD)

        arrive(BLOW, k)
        arrive(BHIGH, k)

        @pl.when(k + AHEAD < CHUNKS)
        def _():
            start(BHIGH, k + AHEAD)
            start(BLOW, k + AHEAD)

        rows = pl.ds(pl.multiple_of(k * ROWS, ROWS), ROWS)
        sums_out[rows] = (
            m_low * blow[rows].astype(F32) + m_high * bhigh[rows].astype(F32)
        ).astype(BF16)
        start(SUMS, k)

        for stage_at, action in zip(STAGES, (partial_sums, correlate, couple)):

            @pl.when(k == stage_at)
            def _():
                action()

        j = k - LAG_SUM

        @pl.when(jnp.logical_and(j >= 0, j % PER == PER - 1))
        def _():
            with_sums(j // PER)

        i = k - LAG_OWN

        @pl.when(jnp.logical_and(i >= 0, i % PER == PER - 1))
        def _():
            with_sides(i // PER)

    groups = CHUNKS // PER
    for group in range((CHUNKS - LAG_SUM) // PER, groups):
        with_sums(group, group == groups - 1)
    for group in range((CHUNKS - LAG_OWN) // PER, groups - 1):
        with_sides(group)

    @pl.loop(0, CHUNKS)
    def _(k):
        for stream in (CROSS, BLOW, BHIGH, SUMS):
            sent(stream, k)

    @pl.loop(0, CHUNKS - PER)
    def _(k):
        for stream in (LOW, HIGH):
            sent(stream, k)

    with_sides(groups - 1, True)
    for k in range(CHUNKS - PER, CHUNKS):
        for stream in (LOW, HIGH):
            sent(stream, k)


def store(total, mixed, d_t, dip, imag, great, out, great_out, left, stage, sems):
    copies = [pltpu.make_async_copy(great, great_out, sems.at[2, 0])]
    blocks = [slice(i * BLOCK, (i + 1) * BLOCK) for i in range(NORB // BLOCK)]
    for i, rows in enumerate(blocks):
        copies.append(pltpu.make_async_copy(imag.at[rows], out.at[1, rows], sems.at[1, i]))
    for copy in copies:
        copy.start()
    left[...] = jnp.dot(mixed[...], d_t[...], preferred_element_type=F32).astype(BF16)
    for i, rows in enumerate(blocks):
        stage[rows, :] = (
            total[rows, :] + jnp.dot(dip[rows, :], left[...], preferred_element_type=F32)
        ).astype(BF16)
        copy = pltpu.make_async_copy(stage.at[rows], out.at[0, rows], sems.at[0, i])
        copy.start()
        copies.append(copy)
    for copy in copies:
        copy.wait()


def in_hbm(x):
    return pltpu.with_memory_space_constraint(x, pltpu.HBM)


def on_device(lesser, great, dipole, weights, flags, lags, strengths, coupling):
    vmem = pl.BlockSpec(memory_space=pltpu.VMEM)
    smem = pltpu.SMEM
    hbm = pl.BlockSpec(memory_space=pltpu.HBM)
    chunks = pltpu.VMEM((NORB, NORB), BF16)
    dma = pltpu.SemaphoreType.DMA
    results = pl.pallas_call(
        body,
        out_shape=(
            pltpu.VMEM((NORB, NORB), F32),
            pltpu.VMEM((TILE, NORB), BF16),
            pltpu.VMEM((NORB, NORB), BF16),
            pltpu.VMEM((NORB, TILE), BF16),
            pltpu.VMEM((NORB, NORB), BF16),
            pltpu.VMEM((8, LANE), F32),
        ),
        in_specs=[hbm] * 4 + [pl.BlockSpec(memory_space=smem)] + [hbm] * 3,
        out_specs=(vmem,) * 6,
        scratch_shapes=[
            pltpu.VMEM((8, LANE), F32), pltpu.VMEM((8, LANE), F32),
            smem((1, 3), F32), smem((MODES,), jnp.int32), smem((2, MODES), F32),
            pltpu.VMEM((2, NORB, NORB), BF16),
            pltpu.VMEM((NORB, NORB), BF16),
            chunks, chunks, chunks, chunks, chunks, chunks, chunks,
            pltpu.VMEM((2, TILE, NORB), BF16),
            pltpu.VMEM((NORB, NORB), F32),
            pltpu.VMEM((16, LANE), F32),
            pltpu.VMEM((RING, 16, LANE), BF16),
            pltpu.VMEM((RING, 16, LANE), F32),
            pltpu.VMEM((RING, 16, LANE), F32),
            pltpu.VMEM((2, 16, LANE), F32),
            pltpu.VMEM((2, 16, LANE), F32),
            pltpu.VMEM((16, LANE), F32),
            pltpu.VMEM((2, 8, LANE), F32),
            pltpu.VMEM((2, 8, LANE), F32),
            dma((6, CHUNKS)), dma((6, CHUNKS)),
            dma((RING,)), dma((RING,)),
            dma((RING,)), dma((RING,)),
            dma((2,)), dma((2,)),
            dma, dma,
            dma((8,)),
        ],
        name="stencil",
        cost_estimate=pl.CostEstimate(
            flops=8 * NORB**3, bytes_accessed=10 * NORB * NORB, transcendentals=0
        ),
        compiler_params=pltpu.CompilerParams(
            collective_id=0, has_side_effects=True, vmem_limit_bytes=40 << 20
        ),
    )(
        in_hbm(lesser.reshape(2, NORB, NORB)), in_hbm(great.reshape(8, LANE)),
        in_hbm(dipole.reshape(NORB, NORB)), in_hbm(weights), flags, in_hbm(lags),
        in_hbm(strengths), in_hbm(coupling.reshape(8, LANE)),
    )
    out, great_out = pl.pallas_call(
        store,
        out_shape=(
            jax.ShapeDtypeStruct((2, NORB, NORB), BF16),
            jax.ShapeDtypeStruct((8, LANE), F32),
        ),
        in_specs=[vmem] * 6,
        out_specs=(hbm, hbm),
        scratch_shapes=[
            pltpu.VMEM((TILE, NORB), BF16),
            pltpu.VMEM((NORB, NORB), BF16),
            dma((3, NORB // BLOCK)),
        ],
        name="store",
        compiler_params=pltpu.CompilerParams(vmem_limit_bytes=8 << 20),
    )(*results)
    return out.reshape(1, 1, 2, NORB, NORB), great_out.reshape(1, 1, NORB)


def solution(mesh):
    return jax.shard_map(
        on_device,
        mesh=mesh,
        in_specs=(
            P("energy", "slab", None, None, None),
            P("energy", "slab", None),
            P("slab", None, None),
            P("energy", None),
            P("energy"),
            P(),
            P(),
            P("slab", None),
        ),
        out_specs=(P("energy", "slab", None, None, None), P("energy", "slab", None)),
        check_vma=False,
    )
```

```python
import jax
import jax.numpy as jnp
from jax import lax
from jax.experimental import pallas as pl
from jax.experimental.pallas import tpu as pltpu
from jax.sharding import PartitionSpec as P

F32, BF16 = jnp.float32, jnp.bfloat16
MESH = pl.DeviceIdType.MESH

RING = 8
LAYERS = 4
CHAIN = RING * LAYERS
SLABS = 4
MODES = 6
NORB = 1024
ROWS = 128
CHUNKS = NORB // ROWS
TILE = 128
PER = TILE // ROWS
AHEAD = 5
AHEAD_CROSS = 2
LAG_SUM = 1
LAG_OWN = 6
STAGES = (3, 4, 5)
BLOCK = 256
LANE = 128

CROSS, LOW, HIGH, BLOW, BHIGH, SUMS = range(6)


def body(
    lesser, great_in, dip, weights_in, flags, lags_in, strengths_in, coupling_in,
    total_real, mixed_last, d_t, d_last, out_imag, great_out,
    great, coupling, weights, lags, strengths, g_v, d_v, crossed, low, high, blow, bhigh, sums, sums_out, left, total_imag,
    diagonal, zbuf, pbuf, qbuf, nbuf, nsend, phon, wsend, wrecv,
    send, recv, zs, zr, ps, pr, ns, nr, ws, wr, local,
):
    e = lax.axis_index("energy")
    s = lax.axis_index("slab")
    w, h = e // 2, e % 2
    y, z = w // RING, w % RING
    mirror = (w * 2 + (1 - h), s)

    def at(chain):
        return (chain * 2 + h, s)

    def inside(chain):
        return jnp.logical_and(chain >= 0, chain < CHAIN)

    a_low, a_high = h - 2, h + 1
    b_low, b_high = -1 - h, 2 - h

    pairs = (
        (weights_in, weights), (great_in, great), (lesser.at[1], g_v.at[1]),
        (lags_in, lags), (strengths_in, strengths), (coupling_in, coupling),
        (lesser.at[0], g_v.at[0]), (dip, d_v),
    )
    copies_in = [pltpu.make_async_copy(*pair, local.at[i]) for i, pair in enumerate(pairs)]

    barrier = pltpu.get_barrier_semaphore()
    expected = jnp.int32(2 * (RING - 1))
    for step in (-2, -1, 1, 2):
        ok = inside(w + step)
        expected = expected + ok.astype(jnp.int32)

        @pl.when(ok)
        def _():
            pl.semaphore_signal(barrier, inc=1, device_id=at(w + step), device_id_type=MESH)

    def ring_mate(d):
        return ((y * RING + (z + d) % RING) * 2 + h, s)

    def plane_mate(t):
        return ((((y + t // 2) % LAYERS) * RING + z) * 2 + (h + t % 2) % 2, s)

    for d in range(1, RING):
        pl.semaphore_signal(barrier, inc=1, device_id=ring_mate(d), device_id_type=MESH)
        pl.semaphore_signal(barrier, inc=1, device_id=plane_mate(d), device_id_type=MESH)
    for step in (-1, 1):
        ok = jnp.logical_and(s + step >= 0, s + step < SLABS)
        expected = expected + ok.astype(jnp.int32)

        @pl.when(ok)
        def _():
            pl.semaphore_signal(barrier, inc=1, device_id=(e, s + step), device_id_type=MESH)

    pl.semaphore_wait(barrier, expected)

    def chunk_copy(stream, k):
        rows = pl.ds(pl.multiple_of(k * ROWS, ROWS), ROWS)
        source, target, device = {
            CROSS: (lesser.at[0, rows], crossed.at[rows], mirror),
            LOW: (crossed.at[rows], low.at[rows], at(w - a_low)),
            HIGH: (crossed.at[rows], high.at[rows], at(w - a_high)),
            BLOW: (lesser.at[1, rows], blow.at[rows], at(w - b_low)),
            BHIGH: (lesser.at[1, rows], bhigh.at[rows], at(w - b_high)),
            SUMS: (sums_out.at[rows], sums.at[rows], mirror),
        }[stream]
        return pltpu.make_async_remote_copy(
            source, target, send.at[stream, k], recv.at[stream, k],
            device_id=device, device_id_type=MESH,
        )

    sends_to = {
        LOW: inside(w - a_low), HIGH: inside(w - a_high),
        BLOW: inside(w - b_low), BHIGH: inside(w - b_high),
    }
    hears = {
        LOW: inside(w + a_low), HIGH: inside(w + a_high),
        BLOW: inside(w + b_low), BHIGH: inside(w + b_high),
    }

    def start(stream, k):
        if stream in sends_to:

            @pl.when(sends_to[stream])
            def _():
                chunk_copy(stream, k).start()
        else:
            chunk_copy(stream, k).start()

    def arrive(stream, k):
        if stream in hears:

            @pl.when(hears[stream])
            def _():
                chunk_copy(stream, k).wait_recv()
        else:
            chunk_copy(stream, k).wait_recv()

    def sent(stream, k):
        if stream in sends_to:

            @pl.when(sends_to[stream])
            def _():
                chunk_copy(stream, k).wait_send()
        else:
            chunk_copy(stream, k).wait_send()

    @pl.loop(0, AHEAD_CROSS)
    def _(k):
        start(CROSS, k)

    @pl.loop(0, AHEAD)
    def _(k):
        start(BHIGH, k)
        start(BLOW, k)

    for copy in copies_in:
        copy.start()
    for copy in copies_in[:3]:
        copy.wait()

    flag = flags[0].astype(F32)
    own_w, low_w, high_w = weights[0, 0], flag * weights[0, 1], flag * weights[0, 2]
    wsend[0] = jnp.full((8, LANE), low_w, F32)
    wsend[1] = jnp.full((8, LANE), high_w, F32)
    weight_copy = pltpu.make_async_remote_copy(
        wsend, wrecv, ws, wr, device_id=mirror, device_id_type=MESH
    )
    weight_copy.start()

    for stream, buffer in ((LOW, low), (HIGH, high), (BLOW, blow), (BHIGH, bhigh)):

        @pl.when(jnp.logical_not(hears[stream]))
        def _():
            @pl.loop(0, NORB // TILE)
            def _(k):
                buffer[pl.ds(pl.multiple_of(k * TILE, TILE), TILE)] = jnp.zeros((TILE, NORB), BF16)

    eye = lax.broadcasted_iota(jnp.int32, (LANE, LANE), 0) == lax.broadcasted_iota(
        jnp.int32, (LANE, LANE), 1
    )
    for b in range(NORB // LANE):
        part = slice(b * LANE, (b + 1) * LANE)
        tile = jnp.where(eye, g_v[1, part, part].astype(F32), 0.0)
        diagonal[b : b + 1, :] = jnp.sum(tile, axis=0, keepdims=True)
    diagonal[8:16, :] = great[...]
    zbuf[0] = diagonal[...].astype(BF16)

    def ring_copy(d):
        return pltpu.make_async_remote_copy(
            zbuf.at[0], zbuf.at[d], zs.at[d], zr.at[d],
            device_id=ring_mate(d), device_id_type=MESH,
        )

    for d in range(1, RING):
        ring_copy(d).start()

    totals = (total_real, total_imag)
    for total in totals:

        @pl.loop(0, NORB // BLOCK)
        def _(i):
            total[pl.ds(i * BLOCK, BLOCK), :] = jnp.zeros((BLOCK, NORB), F32)

    for copy in copies_in[3:]:
        copy.wait()

    @pl.loop(0, NORB // LANE)
    def _(i):
        part = pl.ds(pl.multiple_of(i * LANE, LANE), LANE)
        d_t[:, part] = d_v[part, :].T

    d_last[...] = d_v[:, NORB - TILE :]

    weight_copy.wait()
    m_low, m_high = wrecv[0, 0:1, 0:1], wrecv[1, 0:1, 0:1]

    def plane_copy(t):
        return pltpu.make_async_remote_copy(
            pbuf.at[t], qbuf.at[t], ps.at[t], pr.at[t],
            device_id=plane_mate(t), device_id_type=MESH,
        )

    def partial_sums():
        for d in range(1, RING):
            ring_copy(d).wait()

        @pl.loop(0, RING)
        def _(t):
            row = (((y + t // 2) % LAYERS) * RING + z) * 2 + (h + t % 2) % 2
            less = jnp.zeros((8, LANE), F32)
            more = jnp.zeros((8, LANE), F32)
            for d in range(RING):
                column = (y * RING + (z - d + RING) % RING) * 2 + h
                k_less = jnp.float32(0.0)
                k_great = jnp.float32(0.0)
                for m in range(MODES):
                    up = column - row == lags[m]
                    down = row - column == lags[m]
                    first, second = strengths[0, m], strengths[1, m]
                    k_less += jnp.where(up, first, 0.0) + jnp.where(down, second, 0.0)
                    k_great += jnp.where(up, second, 0.0) + jnp.where(down, first, 0.0)
                held = diagonal[...] if d == 0 else zbuf[d].astype(F32)
                less += k_less * held[0:8]
                more += k_great * held[8:16]
            pbuf[t, 0:8, :] = less
            pbuf[t, 8:16, :] = more

        for t in range(1, RING):
            plane_copy(t).start()

    def neighbour_copy(side):
        return pltpu.make_async_remote_copy(
            nsend.at[side], nbuf.at[side], ns.at[side], nr.at[side],
            device_id=(e, s + 1 - 2 * side), device_id_type=MESH,
        )

    goes_up, goes_down = s + 1 < SLABS, s > 0

    def correlate():
        total = pbuf[0]
        for t in range(1, RING):
            plane_copy(t).wait()
            total += qbuf[t]
        nsend[1] = total
        for part in (slice(0, 8), slice(8, 16)):
            nsend[0, part, :] = coupling[...] * total[part, :]

        @pl.when(goes_up)
        def _():
            neighbour_copy(0).start()

        @pl.when(goes_down)
        def _():
            neighbour_copy(1).start()

        @pl.when(jnp.logical_not(goes_down))
        def _():
            nbuf[0] = jnp.zeros((16, LANE), F32)

        @pl.when(jnp.logical_not(goes_up))
        def _():
            nbuf[1] = jnp.zeros((16, LANE), F32)

    def couple():
        @pl.when(goes_up)
        def _():
            neighbour_copy(0).wait_send()
            neighbour_copy(1).wait_recv()

        @pl.when(goes_down)
        def _():
            neighbour_copy(1).wait_send()
            neighbour_copy(0).wait_recv()

        for part in (slice(0, 8), slice(8, 16)):
            phon[part, :] = nsend[1, part, :] + nbuf[0, part, :] + coupling[...] * nbuf[1, part, :]
        great_out[...] = phon[8:16, :]

    def multiply(c, tile, mixed, last):
        if last and c == 0:
            mixed_last[...] = mixed
            return
        left[c] = jnp.dot(mixed, d_t[...], preferred_element_type=F32).astype(BF16)

        @pl.loop(0, NORB // BLOCK)
        def _(i):
            rows = pl.ds(pl.multiple_of(i * BLOCK, BLOCK), BLOCK)
            total = totals[c][rows, :] + jnp.dot(
                d_v[rows, tile], left[c], preferred_element_type=F32
            )
            totals[c][rows, :] = total
            if last:
                out_imag[rows, :] = total.astype(BF16)

        if last:
            for i in range(NORB // LANE):
                rows = slice(i * LANE, (i + 1) * LANE)
                out_imag[rows, rows] = (
                    total_imag[rows, rows] + jnp.where(eye, phon[i : i + 1, :], 0.0)
                ).astype(BF16)

    def with_sums(group, last=False):
        for i in range(PER):
            arrive(SUMS, group * PER + i)
        tile = pl.ds(pl.multiple_of(group * TILE, TILE), TILE)
        mixed = own_w * g_v[1, tile].astype(F32) + sums[tile].astype(F32)
        multiply(1, tile, mixed.astype(BF16), last)

    def with_sides(group, last=False):
        for i in range(PER):
            arrive(LOW, group * PER + i)
            arrive(HIGH, group * PER + i)
        tile = pl.ds(pl.multiple_of(group * TILE, TILE), TILE)
        mixed = (
            own_w * g_v[0, tile].astype(F32)
            + low_w * low[tile].astype(F32)
            + high_w * high[tile].astype(F32)
        )
        multiply(0, tile, mixed.astype(BF16), last)

    @pl.loop(0, CHUNKS)
    def _(k):
        arrive(CROSS, k)
        start(HIGH, k)
        start(LOW, k)

        @pl.when(k + AHEAD_CROSS < CHUNKS)
        def _():
            start(CROSS, k + AHEAD_CROSS)

        arrive(BLOW, k)
        arrive(BHIGH, k)

        @pl.when(k + AHEAD < CHUNKS)
        def _():
            start(BHIGH, k + AHEAD)
            start(BLOW, k + AHEAD)

        rows = pl.ds(pl.multiple_of(k * ROWS, ROWS), ROWS)
        sums_out[rows] = (
            m_low * blow[rows].astype(F32) + m_high * bhigh[rows].astype(F32)
        ).astype(BF16)
        start(SUMS, k)

        for stage_at, action in zip(STAGES, (partial_sums, correlate, couple)):

            @pl.when(k == stage_at)
            def _():
                action()

        j = k - LAG_SUM

        @pl.when(jnp.logical_and(j >= 0, j % PER == PER - 1))
        def _():
            with_sums(j // PER)

        i = k - LAG_OWN

        @pl.when(jnp.logical_and(i >= 0, i % PER == PER - 1))
        def _():
            with_sides(i // PER)

    groups = CHUNKS // PER
    for group in range((CHUNKS - LAG_SUM) // PER, groups):
        with_sums(group, group == groups - 1)
    for group in range((CHUNKS - LAG_OWN) // PER, groups - 1):
        with_sides(group)

    @pl.loop(0, CHUNKS)
    def _(k):
        for stream in (CROSS, BLOW, BHIGH, SUMS):
            sent(stream, k)

    @pl.loop(0, CHUNKS - PER)
    def _(k):
        for stream in (LOW, HIGH):
            sent(stream, k)

    with_sides(groups - 1, True)
    for k in range(CHUNKS - PER, CHUNKS):
        for stream in (LOW, HIGH):
            sent(stream, k)


def store(total, mixed, d_t, dip, imag, great, out, great_out, left, stage, sems):
    copies = [pltpu.make_async_copy(great, great_out, sems.at[2, 0])]
    blocks = [slice(i * BLOCK, (i + 1) * BLOCK) for i in range(NORB // BLOCK)]
    for i, rows in enumerate(blocks):
        copies.append(pltpu.make_async_copy(imag.at[rows], out.at[1, rows], sems.at[1, i]))
    for copy in copies:
        copy.start()
    left[...] = jnp.dot(mixed[...], d_t[...], preferred_element_type=F32).astype(BF16)
    for i, rows in enumerate(blocks):
        stage[rows, :] = (
            total[rows, :] + jnp.dot(dip[rows, :], left[...], preferred_element_type=F32)
        ).astype(BF16)
        copy = pltpu.make_async_copy(stage.at[rows], out.at[0, rows], sems.at[0, i])
        copy.start()
        copies.append(copy)
    for copy in copies:
        copy.wait()


def in_hbm(x):
    return pltpu.with_memory_space_constraint(x, pltpu.HBM)


def on_device(lesser, great, dipole, weights, flags, lags, strengths, coupling):
    vmem = pl.BlockSpec(memory_space=pltpu.VMEM)
    smem = pltpu.SMEM
    hbm = pl.BlockSpec(memory_space=pltpu.HBM)
    chunks = pltpu.VMEM((NORB, NORB), BF16)
    dma = pltpu.SemaphoreType.DMA
    results = pl.pallas_call(
        body,
        out_shape=(
            pltpu.VMEM((NORB, NORB), F32),
            pltpu.VMEM((TILE, NORB), BF16),
            pltpu.VMEM((NORB, NORB), BF16),
            pltpu.VMEM((NORB, TILE), BF16),
            pltpu.VMEM((NORB, NORB), BF16),
            pltpu.VMEM((8, LANE), F32),
        ),
        in_specs=[hbm] * 4 + [pl.BlockSpec(memory_space=smem)] + [hbm] * 3,
        out_specs=(vmem,) * 6,
        scratch_shapes=[
            pltpu.VMEM((8, LANE), F32), pltpu.VMEM((8, LANE), F32),
            smem((1, 3), F32), smem((MODES,), jnp.int32), smem((2, MODES), F32),
            pltpu.VMEM((2, NORB, NORB), BF16),
            pltpu.VMEM((NORB, NORB), BF16),
            chunks, chunks, chunks, chunks, chunks, chunks, chunks,
            pltpu.VMEM((2, TILE, NORB), BF16),
            pltpu.VMEM((NORB, NORB), F32),
            pltpu.VMEM((16, LANE), F32),
            pltpu.VMEM((RING, 16, LANE), BF16),
            pltpu.VMEM((RING, 16, LANE), F32),
            pltpu.VMEM((RING, 16, LANE), F32),
            pltpu.VMEM((2, 16, LANE), F32),
            pltpu.VMEM((2, 16, LANE), F32),
            pltpu.VMEM((16, LANE), F32),
            pltpu.VMEM((2, 8, LANE), F32),
            pltpu.VMEM((2, 8, LANE), F32),
            dma((6, CHUNKS)), dma((6, CHUNKS)),
            dma((RING,)), dma((RING,)),
            dma((RING,)), dma((RING,)),
            dma((2,)), dma((2,)),
            dma, dma,
            dma((8,)),
        ],
        name="stencil",
        cost_estimate=pl.CostEstimate(
            flops=8 * NORB**3, bytes_accessed=10 * NORB * NORB, transcendentals=0
        ),
        compiler_params=pltpu.CompilerParams(
            collective_id=0, has_side_effects=True, vmem_limit_bytes=40 << 20
        ),
    )(
        in_hbm(lesser.reshape(2, NORB, NORB)), in_hbm(great.reshape(8, LANE)),
        in_hbm(dipole.reshape(NORB, NORB)), in_hbm(weights), flags, in_hbm(lags),
        in_hbm(strengths), in_hbm(coupling.reshape(8, LANE)),
    )
    out, great_out = pl.pallas_call(
        store,
        out_shape=(
            jax.ShapeDtypeStruct((2, NORB, NORB), BF16),
            jax.ShapeDtypeStruct((8, LANE), F32),
        ),
        in_specs=[vmem] * 6,
        out_specs=(hbm, hbm),
        scratch_shapes=[
            pltpu.VMEM((TILE, NORB), BF16),
            pltpu.VMEM((NORB, NORB), BF16),
            dma((3, NORB // BLOCK)),
        ],
        name="store",
        compiler_params=pltpu.CompilerParams(vmem_limit_bytes=8 << 20),
    )(*results)
    return out.reshape(1, 1, 2, NORB, NORB), great_out.reshape(1, 1, NORB)


def solution(mesh):
    return jax.shard_map(
        on_device,
        mesh=mesh,
        in_specs=(
            P("energy", "slab", None, None, None),
            P("energy", "slab", None),
            P("slab", None, None),
            P("energy", None),
            P("energy"),
            P(),
            P(),
            P("slab", None),
        ),
        out_specs=(P("energy", "slab", None, None, None), P("energy", "slab", None)),
        check_vma=False,
    )
```

```python
import jax
import jax.numpy as jnp
from jax import lax
from jax.experimental import pallas as pl
from jax.experimental.pallas import tpu as pltpu
from jax.sharding import PartitionSpec as P

F32, BF16 = jnp.float32, jnp.bfloat16
MESH = pl.DeviceIdType.MESH

RING = 8
LAYERS = 4
CHAIN = RING * LAYERS
SLABS = 4
MODES = 6
NORB = 1024
ROWS = 128
CHUNKS = NORB // ROWS
TILE = 128
PER = TILE // ROWS
AHEAD = 5
LAG_SUM = 3
LAG_OWN = 7
STAGES = (3, 4, 5)
BLOCK = 256
LANE = 128

CROSS, LOW, HIGH, BLOW, BHIGH, SUMS = range(6)


def body(
    lesser, great_in, dip, weights_in, flags, lags_in, strengths_in, coupling_in,
    total_real, mixed_last, d_t, d_last, out_imag, great_out,
    great, coupling, weights, lags, strengths, g_v, d_v, crossed, low, high, blow, bhigh, sums, sums_out, left, total_imag,
    diagonal, zbuf, pbuf, qbuf, nbuf, nsend, phon, wsend, wrecv,
    send, recv, zs, zr, ps, pr, ns, nr, ws, wr, local,
):
    e = lax.axis_index("energy")
    s = lax.axis_index("slab")
    w, h = e // 2, e % 2
    y, z = w // RING, w % RING
    mirror = (w * 2 + (1 - h), s)

    def at(chain):
        return (chain * 2 + h, s)

    def inside(chain):
        return jnp.logical_and(chain >= 0, chain < CHAIN)

    a_low, a_high = h - 2, h + 1
    b_low, b_high = -1 - h, 2 - h

    pairs = (
        (weights_in, weights), (great_in, great), (lesser.at[1], g_v.at[1]),
        (lags_in, lags), (strengths_in, strengths), (coupling_in, coupling),
        (lesser.at[0], g_v.at[0]), (dip, d_v),
    )
    copies_in = [pltpu.make_async_copy(*pair, local.at[i]) for i, pair in enumerate(pairs)]

    barrier = pltpu.get_barrier_semaphore()
    expected = jnp.int32(2 * (RING - 1))
    for step in (-2, -1, 1, 2):
        ok = inside(w + step)
        expected = expected + ok.astype(jnp.int32)

        @pl.when(ok)
        def _():
            pl.semaphore_signal(barrier, inc=1, device_id=at(w + step), device_id_type=MESH)

    def ring_mate(d):
        return ((y * RING + (z + d) % RING) * 2 + h, s)

    def plane_mate(t):
        return ((((y + t // 2) % LAYERS) * RING + z) * 2 + (h + t % 2) % 2, s)

    for d in range(1, RING):
        pl.semaphore_signal(barrier, inc=1, device_id=ring_mate(d), device_id_type=MESH)
        pl.semaphore_signal(barrier, inc=1, device_id=plane_mate(d), device_id_type=MESH)
    for step in (-1, 1):
        ok = jnp.logical_and(s + step >= 0, s + step < SLABS)
        expected = expected + ok.astype(jnp.int32)

        @pl.when(ok)
        def _():
            pl.semaphore_signal(barrier, inc=1, device_id=(e, s + step), device_id_type=MESH)

    pl.semaphore_wait(barrier, expected)

    def chunk_copy(stream, k):
        rows = pl.ds(pl.multiple_of(k * ROWS, ROWS), ROWS)
        source, target, device = {
            CROSS: (lesser.at[0, rows], crossed.at[rows], mirror),
            LOW: (crossed.at[rows], low.at[rows], at(w - a_low)),
            HIGH: (crossed.at[rows], high.at[rows], at(w - a_high)),
            BLOW: (lesser.at[1, rows], blow.at[rows], at(w - b_low)),
            BHIGH: (lesser.at[1, rows], bhigh.at[rows], at(w - b_high)),
            SUMS: (sums_out.at[rows], sums.at[rows], mirror),
        }[stream]
        return pltpu.make_async_remote_copy(
            source, target, send.at[stream, k], recv.at[stream, k],
            device_id=device, device_id_type=MESH,
        )

    sends_to = {
        LOW: inside(w - a_low), HIGH: inside(w - a_high),
        BLOW: inside(w - b_low), BHIGH: inside(w - b_high),
    }
    hears = {
        LOW: inside(w + a_low), HIGH: inside(w + a_high),
        BLOW: inside(w + b_low), BHIGH: inside(w + b_high),
    }

    def start(stream, k):
        if stream in sends_to:

            @pl.when(sends_to[stream])
            def _():
                chunk_copy(stream, k).start()
        else:
            chunk_copy(stream, k).start()

    def arrive(stream, k):
        if stream in hears:

            @pl.when(hears[stream])
            def _():
                chunk_copy(stream, k).wait_recv()
        else:
            chunk_copy(stream, k).wait_recv()

    def sent(stream, k):
        if stream in sends_to:

            @pl.when(sends_to[stream])
            def _():
                chunk_copy(stream, k).wait_send()
        else:
            chunk_copy(stream, k).wait_send()

    @pl.loop(0, AHEAD)
    def _(k):
        start(CROSS, k)
        start(BHIGH, k)
        start(BLOW, k)

    for copy in copies_in:
        copy.start()
    for copy in copies_in[:3]:
        copy.wait()

    flag = flags[0].astype(F32)
    own_w, low_w, high_w = weights[0, 0], flag * weights[0, 1], flag * weights[0, 2]
    wsend[0] = jnp.full((8, LANE), low_w, F32)
    wsend[1] = jnp.full((8, LANE), high_w, F32)
    weight_copy = pltpu.make_async_remote_copy(
        wsend, wrecv, ws, wr, device_id=mirror, device_id_type=MESH
    )
    weight_copy.start()

    for stream, buffer in ((LOW, low), (HIGH, high), (BLOW, blow), (BHIGH, bhigh)):

        @pl.when(jnp.logical_not(hears[stream]))
        def _():
            @pl.loop(0, NORB // TILE)
            def _(k):
                buffer[pl.ds(pl.multiple_of(k * TILE, TILE), TILE)] = jnp.zeros((TILE, NORB), BF16)

    eye = lax.broadcasted_iota(jnp.int32, (LANE, LANE), 0) == lax.broadcasted_iota(
        jnp.int32, (LANE, LANE), 1
    )
    for b in range(NORB // LANE):
        part = slice(b * LANE, (b + 1) * LANE)
        tile = jnp.where(eye, g_v[1, part, part].astype(F32), 0.0)
        diagonal[b : b + 1, :] = jnp.sum(tile, axis=0, keepdims=True)
    diagonal[8:16, :] = great[...]
    zbuf[0] = diagonal[...].astype(BF16)

    def ring_copy(d):
        return pltpu.make_async_remote_copy(
            zbuf.at[0], zbuf.at[d], zs.at[d], zr.at[d],
            device_id=ring_mate(d), device_id_type=MESH,
        )

    for d in range(1, RING):
        ring_copy(d).start()

    totals = (total_real, total_imag)
    for total in totals:

        @pl.loop(0, NORB // BLOCK)
        def _(i):
            total[pl.ds(i * BLOCK, BLOCK), :] = jnp.zeros((BLOCK, NORB), F32)

    for copy in copies_in[3:]:
        copy.wait()

    @pl.loop(0, NORB // LANE)
    def _(i):
        part = pl.ds(pl.multiple_of(i * LANE, LANE), LANE)
        d_t[:, part] = d_v[part, :].T

    d_last[...] = d_v[:, NORB - TILE :]

    weight_copy.wait()
    m_low, m_high = wrecv[0, 0:1, 0:1], wrecv[1, 0:1, 0:1]

    def plane_copy(t):
        return pltpu.make_async_remote_copy(
            pbuf.at[t], qbuf.at[t], ps.at[t], pr.at[t],
            device_id=plane_mate(t), device_id_type=MESH,
        )

    def partial_sums():
        for d in range(1, RING):
            ring_copy(d).wait()

        @pl.loop(0, RING)
        def _(t):
            row = (((y + t // 2) % LAYERS) * RING + z) * 2 + (h + t % 2) % 2
            less = jnp.zeros((8, LANE), F32)
            more = jnp.zeros((8, LANE), F32)
            for d in range(RING):
                column = (y * RING + (z - d + RING) % RING) * 2 + h
                k_less = jnp.float32(0.0)
                k_great = jnp.float32(0.0)
                for m in range(MODES):
                    up = column - row == lags[m]
                    down = row - column == lags[m]
                    first, second = strengths[0, m], strengths[1, m]
                    k_less += jnp.where(up, first, 0.0) + jnp.where(down, second, 0.0)
                    k_great += jnp.where(up, second, 0.0) + jnp.where(down, first, 0.0)
                held = diagonal[...] if d == 0 else zbuf[d].astype(F32)
                less += k_less * held[0:8]
                more += k_great * held[8:16]
            pbuf[t, 0:8, :] = less
            pbuf[t, 8:16, :] = more

        for t in range(1, RING):
            plane_copy(t).start()

    def neighbour_copy(side):
        return pltpu.make_async_remote_copy(
            nsend.at[side], nbuf.at[side], ns.at[side], nr.at[side],
            device_id=(e, s + 1 - 2 * side), device_id_type=MESH,
        )

    goes_up, goes_down = s + 1 < SLABS, s > 0

    def correlate():
        total = pbuf[0]
        for t in range(1, RING):
            plane_copy(t).wait()
            total += qbuf[t]
        nsend[1] = total
        for part in (slice(0, 8), slice(8, 16)):
            nsend[0, part, :] = coupling[...] * total[part, :]

        @pl.when(goes_up)
        def _():
            neighbour_copy(0).start()

        @pl.when(goes_down)
        def _():
            neighbour_copy(1).start()

        @pl.when(jnp.logical_not(goes_down))
        def _():
            nbuf[0] = jnp.zeros((16, LANE), F32)

        @pl.when(jnp.logical_not(goes_up))
        def _():
            nbuf[1] = jnp.zeros((16, LANE), F32)

    def couple():
        @pl.when(goes_up)
        def _():
            neighbour_copy(0).wait_send()
            neighbour_copy(1).wait_recv()

        @pl.when(goes_down)
        def _():
            neighbour_copy(1).wait_send()
            neighbour_copy(0).wait_recv()

        for part in (slice(0, 8), slice(8, 16)):
            phon[part, :] = nsend[1, part, :] + nbuf[0, part, :] + coupling[...] * nbuf[1, part, :]
        great_out[...] = phon[8:16, :]

    def multiply(c, tile, mixed, last):
        if last and c == 0:
            mixed_last[...] = mixed
            return
        left[c] = jnp.dot(mixed, d_t[...], preferred_element_type=F32).astype(BF16)

        @pl.loop(0, NORB // BLOCK)
        def _(i):
            rows = pl.ds(pl.multiple_of(i * BLOCK, BLOCK), BLOCK)
            total = totals[c][rows, :] + jnp.dot(
                d_v[rows, tile], left[c], preferred_element_type=F32
            )
            totals[c][rows, :] = total
            if last:
                out_imag[rows, :] = total.astype(BF16)

        if last:
            for i in range(NORB // LANE):
                rows = slice(i * LANE, (i + 1) * LANE)
                out_imag[rows, rows] = (
                    total_imag[rows, rows] + jnp.where(eye, phon[i : i + 1, :], 0.0)
                ).astype(BF16)

    def with_sums(group, last=False):
        for i in range(PER):
            arrive(SUMS, group * PER + i)
        tile = pl.ds(pl.multiple_of(group * TILE, TILE), TILE)
        mixed = own_w * g_v[1, tile].astype(F32) + sums[tile].astype(F32)
        multiply(1, tile, mixed.astype(BF16), last)

    def with_sides(group, last=False):
        for i in range(PER):
            arrive(LOW, group * PER + i)
            arrive(HIGH, group * PER + i)
        tile = pl.ds(pl.multiple_of(group * TILE, TILE), TILE)
        mixed = (
            own_w * g_v[0, tile].astype(F32)
            + low_w * low[tile].astype(F32)
            + high_w * high[tile].astype(F32)
        )
        multiply(0, tile, mixed.astype(BF16), last)

    @pl.loop(0, CHUNKS)
    def _(k):
        arrive(CROSS, k)
        start(HIGH, k)
        start(LOW, k)

        @pl.when(k + AHEAD < CHUNKS)
        def _():
            start(CROSS, k + AHEAD)

        arrive(BLOW, k)
        arrive(BHIGH, k)

        @pl.when(k + AHEAD < CHUNKS)
        def _():
            start(BHIGH, k + AHEAD)
            start(BLOW, k + AHEAD)

        rows = pl.ds(pl.multiple_of(k * ROWS, ROWS), ROWS)
        sums_out[rows] = (
            m_low * blow[rows].astype(F32) + m_high * bhigh[rows].astype(F32)
        ).astype(BF16)
        start(SUMS, k)

        for stage_at, action in zip(STAGES, (partial_sums, correlate, couple)):

            @pl.when(k == stage_at)
            def _():
                action()

        j = k - LAG_SUM

        @pl.when(jnp.logical_and(j >= 0, j % PER == PER - 1))
        def _():
            with_sums(j // PER)

        i = k - LAG_OWN

        @pl.when(jnp.logical_and(i >= 0, i % PER == PER - 1))
        def _():
            with_sides(i // PER)

    groups = CHUNKS // PER
    for group in range((CHUNKS - LAG_SUM) // PER, groups):
        with_sums(group, group == groups - 1)
    for group in range((CHUNKS - LAG_OWN) // PER, groups - 1):
        with_sides(group)

    @pl.loop(0, CHUNKS)
    def _(k):
        for stream in (CROSS, BLOW, BHIGH, SUMS):
            sent(stream, k)

    @pl.loop(0, CHUNKS - PER)
    def _(k):
        for stream in (LOW, HIGH):
            sent(stream, k)

    with_sides(groups - 1, True)
    for k in range(CHUNKS - PER, CHUNKS):
        for stream in (LOW, HIGH):
            sent(stream, k)


def store(total, mixed, d_t, dip, imag, great, out, great_out, left, stage, sems):
    copies = [pltpu.make_async_copy(great, great_out, sems.at[2, 0])]
    blocks = [slice(i * BLOCK, (i + 1) * BLOCK) for i in range(NORB // BLOCK)]
    for i, rows in enumerate(blocks):
        copies.append(pltpu.make_async_copy(imag.at[rows], out.at[1, rows], sems.at[1, i]))
    for copy in copies:
        copy.start()
    left[...] = jnp.dot(mixed[...], d_t[...], preferred_element_type=F32).astype(BF16)
    for i, rows in enumerate(blocks):
        stage[rows, :] = (
            total[rows, :] + jnp.dot(dip[rows, :], left[...], preferred_element_type=F32)
        ).astype(BF16)
        copy = pltpu.make_async_copy(stage.at[rows], out.at[0, rows], sems.at[0, i])
        copy.start()
        copies.append(copy)
    for copy in copies:
        copy.wait()


def in_hbm(x):
    return pltpu.with_memory_space_constraint(x, pltpu.HBM)


def on_device(lesser, great, dipole, weights, flags, lags, strengths, coupling):
    vmem = pl.BlockSpec(memory_space=pltpu.VMEM)
    smem = pltpu.SMEM
    hbm = pl.BlockSpec(memory_space=pltpu.HBM)
    chunks = pltpu.VMEM((NORB, NORB), BF16)
    dma = pltpu.SemaphoreType.DMA
    results = pl.pallas_call(
        body,
        out_shape=(
            pltpu.VMEM((NORB, NORB), F32),
            pltpu.VMEM((TILE, NORB), BF16),
            pltpu.VMEM((NORB, NORB), BF16),
            pltpu.VMEM((NORB, TILE), BF16),
            pltpu.VMEM((NORB, NORB), BF16),
            pltpu.VMEM((8, LANE), F32),
        ),
        in_specs=[hbm] * 4 + [pl.BlockSpec(memory_space=smem)] + [hbm] * 3,
        out_specs=(vmem,) * 6,
        scratch_shapes=[
            pltpu.VMEM((8, LANE), F32), pltpu.VMEM((8, LANE), F32),
            smem((1, 3), F32), smem((MODES,), jnp.int32), smem((2, MODES), F32),
            pltpu.VMEM((2, NORB, NORB), BF16),
            pltpu.VMEM((NORB, NORB), BF16),
            chunks, chunks, chunks, chunks, chunks, chunks, chunks,
            pltpu.VMEM((2, TILE, NORB), BF16),
            pltpu.VMEM((NORB, NORB), F32),
            pltpu.VMEM((16, LANE), F32),
            pltpu.VMEM((RING, 16, LANE), BF16),
            pltpu.VMEM((RING, 16, LANE), F32),
            pltpu.VMEM((RING, 16, LANE), F32),
            pltpu.VMEM((2, 16, LANE), F32),
            pltpu.VMEM((2, 16, LANE), F32),
            pltpu.VMEM((16, LANE), F32),
            pltpu.VMEM((2, 8, LANE), F32),
            pltpu.VMEM((2, 8, LANE), F32),
            dma((6, CHUNKS)), dma((6, CHUNKS)),
            dma((RING,)), dma((RING,)),
            dma((RING,)), dma((RING,)),
            dma((2,)), dma((2,)),
            dma, dma,
            dma((8,)),
        ],
        name="stencil",
        cost_estimate=pl.CostEstimate(
            flops=8 * NORB**3, bytes_accessed=10 * NORB * NORB, transcendentals=0
        ),
        compiler_params=pltpu.CompilerParams(
            collective_id=0, has_side_effects=True, vmem_limit_bytes=40 << 20
        ),
    )(
        in_hbm(lesser.reshape(2, NORB, NORB)), in_hbm(great.reshape(8, LANE)),
        in_hbm(dipole.reshape(NORB, NORB)), in_hbm(weights), flags, in_hbm(lags),
        in_hbm(strengths), in_hbm(coupling.reshape(8, LANE)),
    )
    out, great_out = pl.pallas_call(
        store,
        out_shape=(
            jax.ShapeDtypeStruct((2, NORB, NORB), BF16),
            jax.ShapeDtypeStruct((8, LANE), F32),
        ),
        in_specs=[vmem] * 6,
        out_specs=(hbm, hbm),
        scratch_shapes=[
            pltpu.VMEM((TILE, NORB), BF16),
            pltpu.VMEM((NORB, NORB), BF16),
            dma((3, NORB // BLOCK)),
        ],
        name="store",
        compiler_params=pltpu.CompilerParams(vmem_limit_bytes=8 << 20),
    )(*results)
    return out.reshape(1, 1, 2, NORB, NORB), great_out.reshape(1, 1, NORB)


def solution(mesh):
    return jax.shard_map(
        on_device,
        mesh=mesh,
        in_specs=(
            P("energy", "slab", None, None, None),
            P("energy", "slab", None),
            P("slab", None, None),
            P("energy", None),
            P("energy"),
            P(),
            P(),
            P("slab", None),
        ),
        out_specs=(P("energy", "slab", None, None, None), P("energy", "slab", None)),
        check_vma=False,
    )
```
